128 devices in a mesh: dp: 8 (over x, core), resp: 16 (over z, y).
Axes of the slice: x: 4, y: 4, z: 4, core: 2. Of those that a mesh axis runs over, the one named last changes fastest.
Arguments:
- queries: bfloat16 [8, 4096, 4096], P('dp', 'resp'), may hold values from -100 to 100
- response_kv: bfloat16 [8, 4096, 1024], P('dp', 'resp'), may hold values from -8 to 8
- cotangent: bfloat16 [8, 4096, 4096], P('dp', 'resp'), may hold values from -6 to 6
- prompt_kv: bfloat16 [8, 16, 128, 1024], P('dp', 'resp'), may hold values from -6 to 6
- resp_lengths: int32 [8, 16, 4], P('dp', 'resp'), may hold values from 1 to 253, as said below
- resp_prompt: int32 [8, 16, 4], P('dp', 'resp'), may hold values from 0 to 3, as said below
- owners: int32 [8, 4], replicated, may hold values from 0 to 127, as said below
Outputs:
- attn_out: bfloat16 [8, 4096, 4096], P('dp', 'resp')
- grad_queries: bfloat16 [8, 4096, 4096], P('dp', 'resp')
- grad_response_kv: bfloat16 [8, 4096, 1024], P('dp', 'resp')
- grad_prompt_kv: float32 [8, 16, 128, 1024], P('dp', 'resp')
The draws below stay inside these ranges and needn't reach their ends.
Inputs may be any that keep to these rules, and one draw needn't show every extreme that they name: The 32 owners are distinct devices. `resp_prompt`: in each dp row every prompt index names exactly 16 responses. `resp_lengths`: A device's lengths sum to between 128 and 256; in every dp row some device's lengths sum to exactly 256.
All inputs are finite; a program needn't handle non-finite values.
Results may differ from the reference program's by a relative error of at most 0.0055.
Values may be sent and summed in bfloat16 or wider, within the bound.
A program may use at most 128 MiB of HBM per device.

```python
import jax
import jax.numpy as jnp
from jax import lax

KEY_VALUE_HEADS = 4
QUERY_PER_KV = 8
HEAD_SIZE = 128
HQ = 32
F = 1024
TOKEN_SLOTS = 256
LP = 128
RESP_DEV = 4
GROUP = 16
P_ROW = 4
N_DP = 8
N_RESP = 16


def base_keys(key):
    return jax.random.normal(jax.random.fold_in(key, 101), (N_DP, N_RESP * TOKEN_SLOTS, KEY_VALUE_HEADS, HEAD_SIZE), jnp.float32)


def draw_response_kv(key, part):
    shared_prompt = base_keys(key)
    key = jax.random.fold_in(key, 1)
    value_rows = jax.random.normal(key, (N_DP, N_RESP * TOKEN_SLOTS, KEY_VALUE_HEADS, HEAD_SIZE), jnp.float32)
    shared_prompt = jnp.clip(shared_prompt, -8.0, 8.0)
    stacked_rows = jnp.concatenate([shared_prompt.reshape(N_DP, N_RESP * TOKEN_SLOTS, KEY_VALUE_HEADS * HEAD_SIZE), value_rows.reshape(N_DP, N_RESP * TOKEN_SLOTS, KEY_VALUE_HEADS * HEAD_SIZE)], axis=-1)
    return stacked_rows.astype(jnp.bfloat16)


def draw_queries(key, part):
    key = jax.random.fold_in(key, 2)
    drawn_result = jax.random.normal(key, (N_DP, N_RESP * TOKEN_SLOTS, KEY_VALUE_HEADS, QUERY_PER_KV, HEAD_SIZE), jnp.float32)
    drawn_result = jnp.clip(drawn_result, -100.0, 100.0)
    return drawn_result.reshape(N_DP, N_RESP * TOKEN_SLOTS, KEY_VALUE_HEADS * QUERY_PER_KV * HEAD_SIZE).astype(jnp.bfloat16)


def draw_owners(key, part):
    key = jax.random.fold_in(key, 3)
    order = jax.random.permutation(key, N_DP * N_RESP)
    return order[:N_DP * P_ROW].reshape(N_DP, P_ROW).astype(jnp.int32)


def draw_resp_prompt(key, part):
    key = jax.random.fold_in(key, 4)
    row_keys = jax.random.split(key, N_DP)
    orders = jax.vmap(lambda sub_key: jax.random.permutation(sub_key, N_RESP * RESP_DEV))(row_keys)
    return (orders // GROUP).reshape(N_DP, N_RESP, RESP_DEV).astype(jnp.int32)


def draw_resp_lengths(key, part):
    key = jax.random.fold_in(key, 5)
    key_total, key_full, key_weight, key_long = jax.random.split(key, 4)
    totals = jax.random.randint(key_total, (N_DP, N_RESP), TOKEN_SLOTS // 2, TOKEN_SLOTS + 1, dtype=jnp.int32)
    full_at = jax.random.randint(key_full, (N_DP, 1), 0, N_RESP, dtype=jnp.int32)
    is_full = jnp.arange(N_RESP, dtype=jnp.int32)[None, :] == full_at
    totals = jnp.where(is_full, TOKEN_SLOTS, totals)
    weights = jax.random.randint(key_weight, (N_DP, N_RESP, RESP_DEV), 1, 17, dtype=jnp.int32)
    shares = (totals[..., None] - RESP_DEV) * weights // jnp.sum(weights, axis=-1, keepdims=True)
    lengths = 1 + shares
    lengths = lengths.at[..., -1].add(totals - jnp.sum(lengths, axis=-1))
    long_at = jax.random.randint(key_long, (N_DP, 1, 1), 0, RESP_DEV, dtype=jnp.int32)
    slot_ids = jnp.arange(RESP_DEV, dtype=jnp.int32)[None, None, :]
    full_lengths = jnp.where(slot_ids == long_at, TOKEN_SLOTS - RESP_DEV + 1, 1)
    lengths = jnp.where(is_full[..., None], full_lengths, lengths)
    return lengths.astype(jnp.int32)


def level_of(stream_key, extent, cuts, least, largest):
    gain = 1.0
    for axis_at, blocks in cuts:
        steps = jax.random.uniform(jax.random.fold_in(jax.random.fold_in(stream_key, 6), axis_at), (blocks,), jnp.float32, least / len(cuts), largest / len(cuts))
        gain = gain * jnp.repeat(jnp.exp(steps), extent[axis_at] // blocks).reshape((-1,) + (1,) * (len(extent) - 1 - axis_at))
    return gain


def scatter_about(own_key, dims, width, reach, shards=(), held_as=jnp.bfloat16):
    entries = width * jax.random.normal(own_key, dims, jnp.float32)
    if shards:
        entries = entries * level_of(own_key, dims, shards, -0.22, 0.18)
    return jnp.clip(entries, -reach, reach).astype(held_as)


def setup_inputs(seed: int = 0) -> dict:
    keys = jax.random.split(jax.random.key(seed), 8)
    return {
        "queries": draw_queries(jax.random.fold_in(keys[7], 71), 0),
        "response_kv": draw_response_kv(jax.random.fold_in(keys[7], 71), 0),
        "cotangent": scatter_about(keys[2], (N_DP, N_RESP * TOKEN_SLOTS, HQ * HEAD_SIZE), 1.0, 6.0, ((0, 8), (1, 16))),
        "prompt_kv": scatter_about(keys[3], (N_DP, N_RESP, LP, F), 1.0, 6.0, ((0, 8), (1, 16))),
        "resp_lengths": draw_resp_lengths(jax.random.fold_in(keys[7], 71), 0),
        "resp_prompt": draw_resp_prompt(jax.random.fold_in(keys[7], 71), 0),
        "owners": draw_owners(jax.random.fold_in(keys[7], 71), 0),
    }


def local_attention(queries, response_kv, cotangent, prompts, lengths, owner_of):
    tok_count = queries.shape[0]
    prompt_count, prompt_len, feature = prompts.shape
    kv_heads = feature // (2 * HEAD_SIZE)
    half_width = kv_heads * HEAD_SIZE
    score_scale = HEAD_SIZE ** -0.5
    ends = jnp.cumsum(lengths).astype(jnp.int32)
    starts = ends - lengths
    places = jnp.arange(tok_count, dtype=jnp.int32)
    inside = (places[:, None] >= starts[None, :]) & (places[:, None] < ends[None, :])
    live_slot = jnp.any(inside, axis=1)
    resp_index = jnp.sum(jnp.where(inside, jnp.arange(lengths.shape[0], dtype=jnp.int32)[None, :], 0), axis=1)
    resp_index = jnp.where(live_slot, resp_index, -1)
    prompt_of = jnp.sum(jnp.where(inside, owner_of[None, :], 0), axis=1)
    key_prompt = jnp.arange(prompt_count * prompt_len, dtype=jnp.int32) // prompt_len
    mask_prompt = (key_prompt[None, :] == prompt_of[:, None]) & live_slot[:, None]
    mask_self = (resp_index[None, :] == resp_index[:, None]) & (places[None, :] <= places[:, None]) & live_slot[:, None]
    allowed = jnp.concatenate([mask_prompt, mask_self], axis=1)
    live_float = live_slot.astype(jnp.float32)
    masked = jnp.where(live_slot[:, None], cotangent, jnp.zeros_like(cotangent))
    heads_q = queries.reshape(tok_count, kv_heads, QUERY_PER_KV, HEAD_SIZE).transpose(1, 0, 2, 3)
    heads_d = masked.reshape(tok_count, kv_heads, QUERY_PER_KV, HEAD_SIZE).transpose(1, 0, 2, 3)
    keys_all = jnp.concatenate([prompts[:, :, :half_width].reshape(prompt_count * prompt_len, kv_heads, HEAD_SIZE),
                                response_kv[:, :half_width].reshape(tok_count, kv_heads, HEAD_SIZE)], axis=0).transpose(1, 0, 2)
    values_all = jnp.concatenate([prompts[:, :, half_width:].reshape(prompt_count * prompt_len, kv_heads, HEAD_SIZE),
                                  response_kv[:, half_width:].reshape(tok_count, kv_heads, HEAD_SIZE)], axis=0).transpose(1, 0, 2)

    def one_head(parts):
        head_queries, head_keys, head_values, head_grad = [part.astype(jnp.float32) for part in parts]
        scores = jnp.einsum('tgd,kd->tgk', head_queries, head_keys) * score_scale
        scores = jnp.where(allowed[:, None, :], scores, -1e30)
        row_max = jnp.max(scores, axis=-1, keepdims=True)
        weights_raw = jnp.exp(scores - row_max)
        weights = weights_raw / jnp.sum(weights_raw, axis=-1, keepdims=True)
        weights_low = lax.optimization_barrier(weights.astype(jnp.bfloat16)).astype(jnp.float32)
        mixed = jnp.einsum('tgk,kd->tgd', weights_low, head_values)
        head_out = (mixed * live_float[:, None, None]).astype(jnp.bfloat16)
        grad_weights = jnp.einsum('tgd,kd->tgk', head_grad, head_values)
        row_delta = jnp.sum(weights * grad_weights, axis=-1, keepdims=True)
        grad_scores = (weights * (grad_weights - row_delta)).astype(jnp.bfloat16)
        grad_scores = lax.optimization_barrier(grad_scores).astype(jnp.float32)
        grad_head_q = (jnp.einsum('tgk,kd->tgd', grad_scores, head_keys) * score_scale).astype(jnp.bfloat16)
        grad_keys = jnp.einsum('tgk,tgd->kd', grad_scores, head_queries) * score_scale
        grad_values = jnp.einsum('tgk,tgd->kd', weights_low, head_grad)
        return head_out, grad_head_q, grad_keys, grad_values

    out_heads, grad_q_heads, grad_keys, grad_values = lax.map(one_head, (heads_q, keys_all, values_all, heads_d))
    attn_out = out_heads.transpose(1, 0, 2, 3).reshape(tok_count, -1)
    grad_queries = grad_q_heads.transpose(1, 0, 2, 3).reshape(tok_count, -1)
    key_total = prompt_count * prompt_len
    grad_keys = grad_keys.transpose(1, 0, 2).reshape(key_total + tok_count, half_width)
    grad_values = grad_values.transpose(1, 0, 2).reshape(key_total + tok_count, half_width)
    grad_response = jnp.concatenate([grad_keys[key_total:], grad_values[key_total:]], axis=1).astype(jnp.bfloat16)
    grad_prompts = jnp.concatenate([grad_keys[:key_total], grad_values[:key_total]], axis=1).reshape(prompt_count, prompt_len, feature)
    return attn_out, grad_queries, grad_response, grad_prompts


def reference(queries, response_kv, cotangent, prompt_kv, resp_lengths, resp_prompt, owners):
    device_total = N_DP * N_RESP
    owned = prompt_kv.reshape(device_total, LP, F)[owners]
    query_rows = queries.reshape(N_DP, N_RESP, TOKEN_SLOTS, HQ * HEAD_SIZE)
    kv_rows = response_kv.reshape(N_DP, N_RESP, TOKEN_SLOTS, F)
    grad_rows = cotangent.reshape(N_DP, N_RESP, TOKEN_SLOTS, HQ * HEAD_SIZE)

    def per_row(items):
        row_queries, row_kv, row_grad, row_lengths, row_prompt, row_prompts = items

        def per_device(running, device_items):
            dev_queries, dev_kv, dev_grad, dev_lengths, dev_prompt = device_items
            result = local_attention(dev_queries, dev_kv, dev_grad, row_prompts, dev_lengths, dev_prompt)
            return running + result[3], (result[0], result[1], result[2])

        running, stacked_rows = lax.scan(per_device, jnp.zeros((P_ROW, LP, F), jnp.float32),
                                    (row_queries, row_kv, row_grad, row_lengths, row_prompt))
        return stacked_rows[0], stacked_rows[1], stacked_rows[2], running

    attn_out, grad_queries, grad_response, totals = lax.map(
        per_row, (query_rows, kv_rows, grad_rows, resp_lengths, resp_prompt, owned))
    grad_prompt_kv = jnp.zeros((device_total, LP, F), jnp.float32).at[owners.reshape(-1)].set(
        totals.reshape(N_DP * P_ROW, LP, F)).reshape(N_DP, N_RESP, LP, F)
    return (attn_out.reshape(N_DP, N_RESP * TOKEN_SLOTS, HQ * HEAD_SIZE),
            grad_queries.reshape(N_DP, N_RESP * TOKEN_SLOTS, HQ * HEAD_SIZE),
            grad_response.reshape(N_DP, N_RESP * TOKEN_SLOTS, F),
            grad_prompt_kv)
```

```python
import jax
import jax.numpy as jnp
from jax import lax
from jax.experimental import pallas as pl
from jax.experimental.pallas import tpu as pltpu
from jax.sharding import PartitionSpec as P

F32 = jnp.float32
BF16 = jnp.bfloat16
HEAD = 128
QPK = 8
KVH = 4
TOK = 256
LP = 128
NP = 4
HALF = KVH * HEAD
NEG = -1e30
SCALE = HEAD ** -0.5
EXP2_SCALE = SCALE * 1.4426950408889634

NN = (((1,), (0,)), ((), ()))
NT = (((1,), (1,)), ((), ()))


def dot(a, b, dims):
    return lax.dot_general(a, b, dims, preferred_element_type=F32)


def cols(index, width=HEAD):
    return pl.ds(pl.multiple_of(index * width, width), width)


def build_masks(len_ref, prm_ref, bias, qmask, lmask):
    def slot_ids(place):
        resp = jnp.full(place.shape, -1, jnp.int32)
        prompt = jnp.full(place.shape, -1, jnp.int32)
        start = jnp.int32(0)
        for i in range(4):
            end = start + len_ref[0, i]
            inside = (place >= start) & (place < end)
            resp = jnp.where(inside, i, resp)
            prompt = jnp.where(inside, prm_ref[0, i], prompt)
            start = end
        return resp, prompt

    keys = lax.broadcasted_iota(jnp.int32, (TOK, TOK), 0)
    slots = lax.broadcasted_iota(jnp.int32, (TOK, TOK), 1)
    key_resp, _ = slot_ids(keys)
    slot_resp, _ = slot_ids(slots)
    allowed = (key_resp == slot_resp) & (keys <= slots) & (slot_resp >= 0)
    bias[...] = jnp.where(allowed, 0.0, NEG)
    _, by_row = slot_ids(lax.broadcasted_iota(jnp.int32, (TOK, HEAD), 0))
    _, by_lane = slot_ids(lax.broadcasted_iota(jnp.int32, (LP, TOK), 1))
    for j in range(NP):
        qmask[j] = jnp.where(by_row == j, 1.0, 0.0).astype(BF16)
        lmask[j] = jnp.where(by_lane == j, 1.0, 0.0).astype(BF16)


def self_scores(n, q_ref, do_ref, kv_ref, bias, e_self, dp_self, stat):
    h = n // QPK
    keys = kv_ref[:, cols(h)]
    values = kv_ref[:, cols(h + KVH)]
    raw = dot(keys, q_ref[:, cols(n)], NT) + bias[...]
    top = jnp.max(raw, axis=0, keepdims=True)
    e = jnp.exp2((raw - top) * EXP2_SCALE)
    dp = dot(values, do_ref[:, cols(n)], NT)
    e_self[n] = e
    dp_self[n] = dp
    stat[n, 0:1, :] = top
    stat[n, 1:2, :] = jnp.sum(e, axis=0, keepdims=True)
    stat[n, 2:3, :] = jnp.sum(e * dp, axis=0, keepdims=True)


def prompt_scores(n, q_ref, do_ref, qmask, kcat, vcat, w_pr, ds_pr, stat, dk_acc, dv_acc):
    h = n // QPK
    q = q_ref[:, cols(n)]
    do = do_ref[:, cols(n)]
    qe = jnp.concatenate([q * qmask[j] for j in range(NP)], axis=1)
    de = jnp.concatenate([do * qmask[j] for j in range(NP)], axis=1)
    raw = dot(kcat[h], qe, NT)
    dp = dot(vcat[h], de, NT)
    top_self = stat[n, 0:1, :]
    top = jnp.maximum(jnp.max(raw, axis=0, keepdims=True), top_self)
    e = jnp.exp2((raw - top) * EXP2_SCALE)
    shrink = jnp.exp2((top_self - top) * EXP2_SCALE)
    total = jnp.sum(e, axis=0, keepdims=True) + shrink * stat[n, 1:2, :]
    inverse = 1.0 / total
    delta = (jnp.sum(e * dp, axis=0, keepdims=True) + shrink * stat[n, 2:3, :]) * inverse
    w = e * inverse
    ds = (w * (dp - delta)).astype(BF16)
    w = w.astype(BF16)
    stat[n, 3:4, :] = shrink * inverse
    stat[n, 4:5, :] = delta
    w_pr[n] = w
    ds_pr[n] = ds
    return dot(ds, qe, NN), dot(w, de, NN)


def finish(n, q_ref, do_ref, lmask, kt, vt, e_self, dp_self, w_pr, ds_pr, stat, out_ref, dq_ref):
    h = n // QPK
    w = e_self[n] * stat[n, 3:4, :]
    ds = (w * (dp_self[n] - stat[n, 4:5, :])).astype(BF16)
    w = w.astype(BF16)
    w_all = jnp.concatenate([w_pr[n] * lmask[j] for j in range(NP)] + [w], axis=0)
    ds_all = jnp.concatenate([ds_pr[n] * lmask[j] for j in range(NP)] + [ds], axis=0)
    out = dot(vt[h], w_all, NN).astype(BF16)
    dq = (dot(kt[h], ds_all, NN) * SCALE).astype(BF16)
    out_ref[:, cols(n)] = out.T
    dq_ref[:, cols(n)] = dq.T
    return dot(ds, q_ref[:, cols(n)], NN), dot(w, do_ref[:, cols(n)], NN)


def prompt_tables(pr_ref, kcat, vcat):
    for h in range(KVH):
        for j in range(NP):
            kcat[h, :, j * HEAD:(j + 1) * HEAD] = pr_ref[j, :, h * HEAD:(h + 1) * HEAD]
            vcat[h, :, j * HEAD:(j + 1) * HEAD] = pr_ref[j, :, HALF + h * HEAD:HALF + (h + 1) * HEAD]


def transposed_tables(pr_ref, kv_ref, kt, vt):
    for h in range(KVH):
        for j in range(NP):
            kt[h, :, j * LP:(j + 1) * LP] = pr_ref[j, :, h * HEAD:(h + 1) * HEAD].T
            vt[h, :, j * LP:(j + 1) * LP] = pr_ref[j, :, HALF + h * HEAD:HALF + (h + 1) * HEAD].T
        kt[h, :, NP * LP:] = kv_ref[:, h * HEAD:(h + 1) * HEAD].T
        vt[h, :, NP * LP:] = kv_ref[:, HALF + h * HEAD:HALF + (h + 1) * HEAD].T


N_DP = 8
N_RESP = 16
CH = 16
HEADS = KVH * QPK
STEP = 2
SELF_CUTS = (0, 10, 20, 32)
FINISH_CUTS = (0, 12, 22, 32)
MESH = pl.DeviceIdType.MESH


def kernel(
    q_hbm, do_hbm, kv_hbm, slot_ref, len_ref, prm_ref, own_ref,
    out_hbm, dq_hbm, gr_hbm, gp_out,
    q_ref, do_ref, kv_ref, out_ref, dq_ref, gr_ref,
    bias, qmask, lmask, e_self, dp_self, stat, kcat, vcat, kt, vt, w_pr, ds_pr, dk_acc, dv_acc, dks, dvs,
    buf1, send2, recv2, mine, pall, gp, gland, gmine, gland2, send3, fin, inv,
    in_sem, out_sem, s1, r1, s2, r2, s3, r3, s4, r4, s5, r5, s6, r6,
):
    a = lax.axis_index("dp")
    c = lax.axis_index("resp")

    loads = [
        pltpu.make_async_copy(src, dst, in_sem.at[i])
        for i, (src, dst) in enumerate(((kv_hbm, kv_ref), (q_hbm, q_ref), (do_hbm, do_ref)))
    ]
    for load in loads:
        load.start()

    def col_peer(d):
        return lax.rem(c + d, N_RESP)

    def row_peer(d):
        return lax.rem(a + d, N_DP)

    def chunk(index):
        half = index // 8
        block = lax.rem(index, 8)
        return pl.ds(pl.multiple_of(block * CH, CH), CH), half

    def chunk_cols(index):
        rows, half = chunk(index)
        return rows, pl.ds(pl.multiple_of(half * HALF, HALF), HALF)

    def send(src, dst, ssem, rsem, device):
        return pltpu.make_async_remote_copy(
            src_ref=src, dst_ref=dst, send_sem=ssem, recv_sem=rsem, device_id=device, device_id_type=MESH
        )

    barrier = pltpu.get_barrier_semaphore()
    for d in range(1, N_RESP):
        pl.semaphore_signal(barrier, inc=1, device_id=(a, col_peer(d)), device_id_type=MESH)
    for d in range(1, N_DP):
        pl.semaphore_signal(barrier, inc=1, device_id=(row_peer(d), c), device_id_type=MESH)
    build_masks(len_ref, prm_ref, bias, qmask, lmask)
    pl.semaphore_wait(barrier, N_RESP - 1 + N_DP - 1)

    sent = []
    first = []
    for d in range(1, N_RESP):
        to = col_peer(d)
        rows, lanes = chunk_cols(to)
        copy = send(slot_ref.at[rows, lanes], buf1.at[d], s1.at[d - 1], r1.at[d - 1], (a, to))
        copy.start()
        first.append(copy)
    rows, lanes = chunk_cols(c)
    buf1[0] = slot_ref[rows, lanes]

    @pl.loop(0, N_RESP)
    def _(d):
        device = a * N_RESP + lax.rem(c + d, N_RESP)
        found = jnp.int32(-1)
        for k in range(N_DP * NP):
            found = jnp.where(own_ref[k // NP, k % NP] == device, k, found)
        inv[d] = found

    for load in loads:
        load.wait()

    def self_part(lo, hi):
        @pl.loop(lo // STEP, hi // STEP)
        def _(i):
            for u in range(STEP):
                self_scores(i * STEP + u, q_ref, do_ref, kv_ref, bias, e_self, dp_self, stat)

    self_part(SELF_CUTS[0], SELF_CUTS[1])

    for copy in first:
        copy.wait_recv()
    second = []
    for d in range(N_DP):
        to = row_peer(d)
        for j in range(NP):
            column = jnp.bitwise_and(own_ref[to, j], N_RESP - 1)
            piece = buf1[lax.rem(c + N_RESP - column, N_RESP)]
            if d == 0:
                recv2[0, j] = piece
            else:
                send2[d - 1, j] = piece
        if d:
            copy = send(send2.at[d - 1], recv2.at[d], s2.at[d - 1], r2.at[d - 1], (to, c))
            copy.start()
            second.append(copy)

    self_part(SELF_CUTS[1], SELF_CUTS[2])

    for copy in second:
        copy.wait_recv()
    rows, lanes = chunk_cols(c)
    for j in range(NP):
        owner_row = jnp.right_shift(own_ref[a, j], 4)
        piece = recv2[lax.rem(a + N_DP - owner_row, N_DP), j]
        mine[j] = piece
        pall[j, rows, lanes] = piece
    third = []
    for d in range(1, N_RESP):
        copy = send(mine, pall.at[:, rows, lanes], s3.at[d - 1], r3.at[d - 1], (a, col_peer(d)))
        copy.start()
        third.append(copy)

    self_part(SELF_CUTS[2], SELF_CUTS[3])

    for d in range(1, N_RESP):
        rows_in, lanes_in = chunk_cols(lax.rem(c + N_RESP - d, N_RESP))
        send(mine, pall.at[:, rows_in, lanes_in], s3.at[d - 1], r3.at[d - 1], (a, col_peer(d))).wait_recv()

    prompt_tables(pall, kcat, vcat)
    fourth = []
    for h in range(KVH):
        dk_acc[h] = jnp.zeros((LP, NP * HEAD), F32)
        dv_acc[h] = jnp.zeros((LP, NP * HEAD), F32)

        @pl.loop(0, QPK // STEP)
        def _(i):
            parts = [
                prompt_scores(h * QPK + i * STEP + u, q_ref, do_ref, qmask, kcat, vcat, w_pr, ds_pr, stat, dk_acc, dv_acc)
                for u in range(STEP)
            ]
            dk_acc[h] += sum(p[0] for p in parts)
            dv_acc[h] += sum(p[1] for p in parts)

        for j in range(NP):
            gp[h, 0, j] = (dk_acc[h, :, j * HEAD:(j + 1) * HEAD] * SCALE).astype(BF16)
            gp[h, 1, j] = dv_acc[h, :, j * HEAD:(j + 1) * HEAD].astype(BF16)
        for d in range(1, N_RESP):
            to = col_peer(d)
            rows_to, half_to = chunk(to)
            copy = send(
                gp.at[h, half_to, :, rows_to, :], gland.at[d - 1, h], s4.at[h, d - 1], r4.at[h, d - 1], (a, to)
            )
            copy.start()
            fourth.append(copy)

    transposed_tables(pall, kv_ref, kt, vt)
    dks[...] = jnp.zeros_like(dks)
    dvs[...] = jnp.zeros_like(dvs)

    def finish_part(lo, hi):
        @pl.loop(lo // STEP, hi // STEP)
        def _(i):
            parts = [
                finish(i * STEP + u, q_ref, do_ref, lmask, kt, vt, e_self, dp_self, w_pr, ds_pr, stat, out_ref, dq_ref)
                for u in range(STEP)
            ]
            h = i * STEP // QPK
            dks[h] += sum(p[0] for p in parts)
            dvs[h] += sum(p[1] for p in parts)

    finish_part(FINISH_CUTS[0], FINISH_CUTS[1])

    for copy in fourth:
        copy.wait_recv()
    rows, half = chunk(c)
    for h in range(KVH):
        for j in range(NP):
            total = gp[h, half, j, rows, :].astype(F32)
            for d in range(1, N_RESP):
                total += gland[d - 1, h, j].astype(F32)
            gmine[h, j] = total.astype(BF16)
    gland2[0] = gmine[...]
    fifth = []
    for d in range(1, N_DP):
        copy = send(gmine, gland2.at[d], s5.at[d - 1], r5.at[d - 1], (row_peer(d), c))
        copy.start()
        fifth.append(copy)

    finish_part(FINISH_CUTS[1], FINISH_CUTS[2])

    for copy in fifth:
        copy.wait_recv()
    sixth = []
    for d in range(N_RESP):
        index = inv[d]
        has = index >= 0
        at = jnp.maximum(index, 0)
        row = jnp.right_shift(at, 2)
        j = jnp.bitwise_and(at, 3)
        for h in range(KVH):
            piece = gland2[lax.rem(a + N_DP - row, N_DP), h, j].astype(F32)
            piece = jnp.where(has, piece, 0.0).astype(BF16)
            if d == 0:
                fin[0, h] = piece
            else:
                send3[d - 1, h] = piece
        if d:
            copy = send(send3.at[d - 1], fin.at[d], s6.at[d - 1], r6.at[d - 1], (a, col_peer(d)))
            copy.start()
            sixth.append(copy)

    finish_part(FINISH_CUTS[2], FINISH_CUTS[3])

    for h in range(KVH):
        gr_ref[:, h * HEAD:(h + 1) * HEAD] = (dks[h] * SCALE).astype(BF16)
        gr_ref[:, HALF + h * HEAD:HALF + (h + 1) * HEAD] = dvs[h].astype(BF16)
    stores = [
        pltpu.make_async_copy(src, dst, out_sem.at[i])
        for i, (src, dst) in enumerate(((out_ref, out_hbm), (dq_ref, dq_hbm), (gr_ref, gr_hbm)))
    ]
    for store in stores:
        store.start()

    for copy in sixth:
        copy.wait_recv()
    for d in range(N_RESP):
        rows_in, half_in = chunk(lax.rem(c + N_RESP - d, N_RESP))
        for h in range(KVH):
            lanes_in = pl.ds(pl.multiple_of(half_in * HALF + h * HEAD, HEAD), HEAD)
            gp_out[rows_in, lanes_in] = fin[d, h].astype(F32)

    for copy in first + second + third + fourth + fifth + sixth:
        copy.wait_send()
    for store in stores:
        store.wait()


def local(queries, response_kv, cotangent, prompt_kv, resp_lengths, resp_prompt, owners):
    vm = pl.BlockSpec(memory_space=pltpu.VMEM)
    sm = pl.BlockSpec(memory_space=pltpu.SMEM)
    hbm = pl.BlockSpec(memory_space=pl.ANY)
    peers = (N_RESP - 1,)
    row_peers = (N_DP - 1,)
    dma = pltpu.SemaphoreType.DMA
    outs = pl.pallas_call(
        kernel,
        in_specs=[hbm, hbm, hbm, vm, sm, sm, sm],
        out_specs=[hbm, hbm, hbm, vm],
        out_shape=[
            jax.ShapeDtypeStruct((TOK, 4096), BF16),
            jax.ShapeDtypeStruct((TOK, 4096), BF16),
            jax.ShapeDtypeStruct((TOK, 1024), BF16),
            jax.ShapeDtypeStruct((LP, 1024), F32),
        ],
        scratch_shapes=[
            pltpu.VMEM((TOK, 4096), BF16),
            pltpu.VMEM((TOK, 4096), BF16),
            pltpu.VMEM((TOK, 1024), BF16),
            pltpu.VMEM((TOK, 4096), BF16),
            pltpu.VMEM((TOK, 4096), BF16),
            pltpu.VMEM((TOK, 1024), BF16),
            pltpu.VMEM((TOK, TOK), F32),
            pltpu.VMEM((NP, TOK, HEAD), BF16),
            pltpu.VMEM((NP, LP, TOK), BF16),
            pltpu.VMEM((HEADS, TOK, TOK), F32),
            pltpu.VMEM((HEADS, TOK, TOK), F32),
            pltpu.VMEM((HEADS, 8, TOK), F32),
            pltpu.VMEM((KVH, LP, NP * HEAD), BF16),
            pltpu.VMEM((KVH, LP, NP * HEAD), BF16),
            pltpu.VMEM((KVH, HEAD, NP * LP + TOK), BF16),
            pltpu.VMEM((KVH, HEAD, NP * LP + TOK), BF16),
            pltpu.VMEM((HEADS, LP, TOK), BF16),
            pltpu.VMEM((HEADS, LP, TOK), BF16),
            pltpu.VMEM((KVH, LP, NP * HEAD), F32),
            pltpu.VMEM((KVH, LP, NP * HEAD), F32),
            pltpu.VMEM((KVH, TOK, HEAD), F32),
            pltpu.VMEM((KVH, TOK, HEAD), F32),
            pltpu.VMEM((N_RESP, CH, HALF), BF16),
            pltpu.VMEM((N_DP - 1, NP, CH, HALF), BF16),
            pltpu.VMEM((N_DP, NP, CH, HALF), BF16),
            pltpu.VMEM((NP, CH, HALF), BF16),
            pltpu.VMEM((NP, LP, 2 * HALF), BF16),
            pltpu.VMEM((KVH, 2, NP, LP, HEAD), BF16),
            pltpu.VMEM((N_RESP - 1, KVH, NP, CH, HEAD), BF16),
            pltpu.VMEM((KVH, NP, CH, HEAD), BF16),
            pltpu.VMEM((N_DP, KVH, NP, CH, HEAD), BF16),
            pltpu.VMEM((N_RESP - 1, KVH, CH, HEAD), BF16),
            pltpu.VMEM((N_RESP, KVH, CH, HEAD), BF16),
            pltpu.SMEM((N_RESP,), jnp.int32),
            dma((3,)), dma((3,)),
            dma(peers), dma(peers),
            dma(row_peers), dma(row_peers),
            dma(peers), dma(peers),
            dma((KVH,) + peers), dma((KVH,) + peers),
            dma(row_peers), dma(row_peers),
            dma(peers), dma(peers),
        ],
        compiler_params=pltpu.CompilerParams(
            collective_id=0, has_side_effects=True, vmem_limit_bytes=56 * 2 ** 20
        ),
        name="grouped_attention",
    )(
        queries[0], cotangent[0], response_kv[0], prompt_kv[0, 0],
        resp_lengths[0], resp_prompt[0], owners,
    )
    attn_out, grad_queries, grad_response, grad_prompt = outs
    return attn_out[None], grad_queries[None], grad_response[None], grad_prompt[None, None]


def solution(mesh):
    placed = (
        P("dp", "resp", None),
        P("dp", "resp", None),
        P("dp", "resp", None),
        P("dp", "resp", None, None),
        P("dp", "resp", None),
        P("dp", "resp", None),
        P(),
    )
    return jax.shard_map(
        local,
        mesh=mesh,
        in_specs=placed,
        out_specs=(
            P("dp", "resp", None),
            P("dp", "resp", None),
            P("dp", "resp", None),
            P("dp", "resp", None, None),
        ),
        check_vma=False,
    )
```

```python
import jax
import jax.numpy as jnp
from jax import lax
from jax.experimental import pallas as pl
from jax.experimental.pallas import tpu as pltpu
from jax.sharding import PartitionSpec as P

F32 = jnp.float32
BF16 = jnp.bfloat16
HEAD = 128
QPK = 8
KVH = 4
TOK = 256
LP = 128
NP = 4
HALF = KVH * HEAD
NEG = -1e30
SCALE = HEAD ** -0.5
EXP2_SCALE = SCALE * 1.4426950408889634

NN = (((1,), (0,)), ((), ()))
NT = (((1,), (1,)), ((), ()))


def dot(a, b, dims):
    return lax.dot_general(a, b, dims, preferred_element_type=F32)


def cols(index, width=HEAD):
    return pl.ds(pl.multiple_of(index * width, width), width)


def build_masks(len_ref, prm_ref, bias, qmask, lmask):
    def slot_ids(place):
        resp = jnp.full(place.shape, -1, jnp.int32)
        prompt = jnp.full(place.shape, -1, jnp.int32)
        start = jnp.int32(0)
        for i in range(4):
            end = start + len_ref[0, i]
            inside = (place >= start) & (place < end)
            resp = jnp.where(inside, i, resp)
            prompt = jnp.where(inside, prm_ref[0, i], prompt)
            start = end
        return resp, prompt

    keys = lax.broadcasted_iota(jnp.int32, (TOK, TOK), 0)
    slots = lax.broadcasted_iota(jnp.int32, (TOK, TOK), 1)
    key_resp, _ = slot_ids(keys)
    slot_resp, _ = slot_ids(slots)
    allowed = (key_resp == slot_resp) & (keys <= slots) & (slot_resp >= 0)
    bias[...] = jnp.where(allowed, 0.0, NEG)
    _, by_row = slot_ids(lax.broadcasted_iota(jnp.int32, (TOK, HEAD), 0))
    _, by_lane = slot_ids(lax.broadcasted_iota(jnp.int32, (LP, TOK), 1))
    for j in range(NP):
        qmask[j] = jnp.where(by_row == j, 1.0, 0.0).astype(BF16)
        lmask[j] = jnp.where(by_lane == j, 1.0, 0.0).astype(BF16)


def self_scores(n, q_ref, do_ref, kv_ref, bias, e_self, dp_self, stat):
    h = n // QPK
    keys = kv_ref[:, cols(h)]
    values = kv_ref[:, cols(h + KVH)]
    raw = dot(keys, q_ref[:, cols(n)], NT) + bias[...]
    top = jnp.max(raw, axis=0, keepdims=True)
    e = jnp.exp2((raw - top) * EXP2_SCALE)
    dp = dot(values, do_ref[:, cols(n)], NT)
    e_self[n] = e
    dp_self[n] = dp
    stat[n, 0:1, :] = top
    stat[n, 1:2, :] = jnp.sum(e, axis=0, keepdims=True)
    stat[n, 2:3, :] = jnp.sum(e * dp, axis=0, keepdims=True)


def prompt_scores(n, q_ref, do_ref, qmask, kvcat, w_pr, ds_pr, stat):
    h = n // QPK
    q = q_ref[:, cols(n)]
    do = do_ref[:, cols(n)]
    qe = jnp.concatenate([q * qmask[j] for j in range(NP)], axis=1)
    de = jnp.concatenate([do * qmask[j] for j in range(NP)], axis=1)
    raw = dot(kvcat[0, h], qe, NT)
    dp = dot(kvcat[1, h], de, NT)
    top_self = stat[n, 0:1, :]
    top = jnp.maximum(jnp.max(raw, axis=0, keepdims=True), top_self)
    e = jnp.exp2((raw - top) * EXP2_SCALE)
    shrink = jnp.exp2((top_self - top) * EXP2_SCALE)
    total = jnp.sum(e, axis=0, keepdims=True) + shrink * stat[n, 1:2, :]
    inverse = 1.0 / total
    delta = (jnp.sum(e * dp, axis=0, keepdims=True) + shrink * stat[n, 2:3, :]) * inverse
    w = e * inverse
    ds = (w * (dp - delta)).astype(BF16)
    w = w.astype(BF16)
    stat[n, 3:4, :] = shrink * inverse
    stat[n, 4:5, :] = delta
    w_pr[n] = w
    ds_pr[n] = ds
    return dot(ds, qe, NN), dot(w, de, NN)


def finish(n, q_ref, do_ref, lmask, kt, vt, e_self, dp_self, w_pr, ds_pr, stat, out_ref, dq_ref):
    h = n // QPK
    w = e_self[n] * stat[n, 3:4, :]
    ds = (w * (dp_self[n] - stat[n, 4:5, :])).astype(BF16)
    w = w.astype(BF16)
    w_all = jnp.concatenate([w_pr[n] * lmask[j] for j in range(NP)] + [w], axis=0)
    ds_all = jnp.concatenate([ds_pr[n] * lmask[j] for j in range(NP)] + [ds], axis=0)
    out = dot(vt[h], w_all, NN).astype(BF16)
    dq = (dot(kt[h], ds_all, NN) * SCALE).astype(BF16)
    out_ref[:, cols(n)] = out.T
    dq_ref[:, cols(n)] = dq.T
    return dot(ds, q_ref[:, cols(n)], NN), dot(w, do_ref[:, cols(n)], NN)


def transposed_tables(kvcat, kv_ref, kt, vt):
    for h in range(KVH):
        for half, table in ((0, kt), (1, vt)):
            for j in range(NP):
                table[h, :, j * LP:(j + 1) * LP] = kvcat[half, h, :, j * HEAD:(j + 1) * HEAD].T
            at = half * HALF + h * HEAD
            table[h, :, NP * LP:] = kv_ref[:, at:at + HEAD].T


N_DP = 8
N_RESP = 16
CH = 16
WIDE = NP * HEAD
HEADS = KVH * QPK
STEP = 2
SELF_CUTS = (0, 10, 20, 32)
FINISH_CUTS = (0, 12, 22, 32)
MESH = pl.DeviceIdType.MESH
SPOTS = sorted(range(1, N_RESP), key=lambda s: -(min(s // 4, 4 - s // 4) + min(s % 4, 4 - s % 4)))
LANES = sorted(range(1, N_DP), key=lambda s: -min(s // 2, 4 - s // 2))


def kernel(
    q_hbm, do_hbm, kv_hbm, slot_ref, len_ref, prm_ref, own_ref,
    out_ref, dq_ref, gr_ref, gp_out,
    q_ref, do_ref, kv_ref,
    bias, qmask, lmask, e_self, dp_self, stat, kvcat, kt, vt, w_pr, ds_pr, dk_acc, dv_acc, dks, dvs,
    buf1, send2, recv2, mine, gp, gland, gmine, gland2, send3, fin, inv,
    in_sem, s1, r1, s2, r2, s3, r3, s4, r4, s5, r5, s6, r6,
):
    a = lax.axis_index("dp")
    c = lax.axis_index("resp")
    x, core = a // 2, lax.rem(a, 2)
    z, y = c // 4, lax.rem(c, 4)

    loads = [
        pltpu.make_async_copy(src, dst, in_sem.at[i])
        for i, (src, dst) in enumerate(((kv_hbm, kv_ref), (q_hbm, q_ref), (do_hbm, do_ref)))
    ]
    for load in loads:
        load.start()

    def col_to(s):
        return lax.rem(z + s // 4, 4) * 4 + lax.rem(y + s % 4, 4)

    def col_from(s):
        return lax.rem(z + 4 - s // 4, 4) * 4 + lax.rem(y + 4 - s % 4, 4)

    def row_to(s):
        return lax.rem(x + s // 2, 4) * 2 + lax.rem(core + s % 2, 2)

    def spot_of(column):
        return lax.rem(z + 4 - jnp.right_shift(column, 2), 4) * 4 + lax.rem(y + 4 - jnp.bitwise_and(column, 3), 4)

    def lane_of(row):
        return lax.rem(x + 4 - jnp.right_shift(row, 1), 4) * 2 + lax.rem(core + 2 - jnp.bitwise_and(row, 1), 2)

    def chunk(index):
        half = index // 8
        block = lax.rem(index, 8)
        return half, pl.ds(pl.multiple_of(block * CH, CH), CH)

    def send(src, dst, ssem, rsem, device):
        return pltpu.make_async_remote_copy(
            src_ref=src, dst_ref=dst, send_sem=ssem, recv_sem=rsem, device_id=device, device_id_type=MESH
        )

    barrier = pltpu.get_barrier_semaphore()
    for s in SPOTS:
        pl.semaphore_signal(barrier, inc=1, device_id=(a, col_to(s)), device_id_type=MESH)
    for s in LANES:
        pl.semaphore_signal(barrier, inc=1, device_id=(row_to(s), c), device_id_type=MESH)
    build_masks(len_ref, prm_ref, bias, qmask, lmask)
    pl.semaphore_wait(barrier, len(SPOTS) + len(LANES))

    my_half, my_rows = chunk(c)

    first = []
    for s in SPOTS:
        to = col_to(s)
        half, rows = chunk(to)
        lanes = pl.ds(pl.multiple_of(half * HALF, HALF), HALF)
        copy = send(slot_ref.at[rows, lanes], buf1.at[s], s1.at[s - 1], r1.at[s - 1], (a, to))
        copy.start()
        first.append(copy)
    buf1[0] = slot_ref[my_rows, pl.ds(pl.multiple_of(my_half * HALF, HALF), HALF)]

    @pl.loop(0, N_RESP)
    def _(s):
        device = a * N_RESP + lax.rem(z + s // 4, 4) * 4 + lax.rem(y + lax.rem(s, 4), 4)
        found = jnp.int32(-1)
        for k in range(N_DP * NP):
            found = jnp.where(own_ref[k % NP, k // NP] == device, k, found)
        inv[s] = found

    for load in loads:
        load.wait()

    def self_part(lo, hi):
        @pl.loop(lo // STEP, hi // STEP)
        def _(i):
            for u in range(STEP):
                self_scores(i * STEP + u, q_ref, do_ref, kv_ref, bias, e_self, dp_self, stat)

    self_part(SELF_CUTS[0], SELF_CUTS[1])

    for copy in first:
        copy.wait_recv()
    second = []
    for s in LANES + [0]:
        to = row_to(s)
        for j in range(NP):
            piece = buf1[spot_of(jnp.bitwise_and(own_ref[j, to], N_RESP - 1))]
            if s == 0:
                recv2[0, j] = piece
            else:
                send2[s - 1, j] = piece
        if s:
            copy = send(send2.at[s - 1], recv2.at[s], s2.at[s - 1], r2.at[s - 1], (to, c))
            copy.start()
            second.append(copy)

    self_part(SELF_CUTS[1], SELF_CUTS[2])

    for copy in second:
        copy.wait_recv()
    for j in range(NP):
        piece = recv2[lane_of(jnp.right_shift(own_ref[j, a], 4)), j]
        for h in range(KVH):
            mine[h, :, j * HEAD:(j + 1) * HEAD] = piece[:, h * HEAD:(h + 1) * HEAD]
    third = []
    for h in range(KVH):
        kvcat[my_half, h, my_rows, :] = mine[h]
        for s in SPOTS:
            copy = send(
                mine.at[h], kvcat.at[my_half, h, my_rows, :], s3.at[h, s - 1], r3.at[h, s - 1], (a, col_to(s))
            )
            copy.start()
            third.append(copy)

    self_part(SELF_CUTS[2], SELF_CUTS[3])

    fourth = []
    for h in range(KVH):
        for s in SPOTS:
            half, rows = chunk(col_from(s))
            send(mine.at[h], kvcat.at[half, h, rows, :], s3.at[h, s - 1], r3.at[h, s - 1], (a, col_to(s))).wait_recv()
        dk_acc[...] = jnp.zeros_like(dk_acc)
        dv_acc[...] = jnp.zeros_like(dv_acc)

        @pl.loop(0, QPK // STEP)
        def _(i):
            parts = [
                prompt_scores(h * QPK + i * STEP + u, q_ref, do_ref, qmask, kvcat, w_pr, ds_pr, stat)
                for u in range(STEP)
            ]
            dk_acc[...] += sum(p[0] for p in parts)
            dv_acc[...] += sum(p[1] for p in parts)

        gp[h, 0] = (dk_acc[...] * SCALE).astype(BF16)
        gp[h, 1] = dv_acc[...].astype(BF16)
        for s in SPOTS:
            to = col_to(s)
            half, rows = chunk(to)
            copy = send(gp.at[h, half, rows, :], gland.at[s - 1, h], s4.at[h, s - 1], r4.at[h, s - 1], (a, to))
            copy.start()
            fourth.append(copy)

    transposed_tables(kvcat, kv_ref, kt, vt)
    dks[...] = jnp.zeros_like(dks)
    dvs[...] = jnp.zeros_like(dvs)

    def finish_part(lo, hi):
        @pl.loop(lo // STEP, hi // STEP)
        def _(i):
            parts = [
                finish(i * STEP + u, q_ref, do_ref, lmask, kt, vt, e_self, dp_self, w_pr, ds_pr, stat, out_ref, dq_ref)
                for u in range(STEP)
            ]
            h = i * STEP // QPK
            dks[h] += sum(p[0] for p in parts)
            dvs[h] += sum(p[1] for p in parts)

    finish_part(FINISH_CUTS[0], FINISH_CUTS[1])

    for copy in fourth:
        copy.wait_recv()
    for h in range(KVH):
        total = gp[h, my_half, my_rows, :].astype(F32)
        for s in SPOTS:
            total += gland[s - 1, h].astype(F32)
        total = total.astype(BF16)
        for j in range(NP):
            gmine[j, h] = total[:, j * HEAD:(j + 1) * HEAD]
    gland2[0] = gmine[...]
    fifth = []
    for s in LANES:
        copy = send(gmine, gland2.at[s], s5.at[s - 1], r5.at[s - 1], (row_to(s), c))
        copy.start()
        fifth.append(copy)

    finish_part(FINISH_CUTS[1], FINISH_CUTS[2])

    for copy in fifth:
        copy.wait_recv()
    sixth = []
    for s in SPOTS + [0]:
        index = inv[s]
        at = jnp.maximum(index, 0)
        piece = gland2[lane_of(jnp.right_shift(at, 2)), jnp.bitwise_and(at, 3)].astype(F32)
        piece = jnp.where(index >= 0, piece, 0.0).astype(BF16)
        if s == 0:
            fin[0] = piece
        else:
            send3[s - 1] = piece
            copy = send(send3.at[s - 1], fin.at[s], s6.at[s - 1], r6.at[s - 1], (a, col_to(s)))
            copy.start()
            sixth.append(copy)

    finish_part(FINISH_CUTS[2], FINISH_CUTS[3])

    for h in range(KVH):
        gr_ref[:, h * HEAD:(h + 1) * HEAD] = (dks[h] * SCALE).astype(BF16)
        gr_ref[:, HALF + h * HEAD:HALF + (h + 1) * HEAD] = dvs[h].astype(BF16)

    for copy in sixth:
        copy.wait_recv()
    for s in range(N_RESP):
        half, rows = chunk(col_from(s))
        for h in range(KVH):
            lanes = pl.ds(pl.multiple_of(half * HALF + h * HEAD, HEAD), HEAD)
            gp_out[rows, lanes] = fin[s, h].astype(F32)

    for copy in first + second + third + fourth + fifth + sixth:
        copy.wait_send()


def local(queries, response_kv, cotangent, prompt_kv, resp_lengths, resp_prompt, owners):
    vm = pl.BlockSpec(memory_space=pltpu.VMEM)
    sm = pl.BlockSpec(memory_space=pltpu.SMEM)
    hbm = pl.BlockSpec(memory_space=pl.ANY)
    peers = (N_RESP - 1,)
    row_peers = (N_DP - 1,)
    dma = pltpu.SemaphoreType.DMA
    outs = pl.pallas_call(
        kernel,
        in_specs=[hbm, hbm, hbm, vm, sm, sm, sm],
        out_specs=[vm] * 4,
        out_shape=[
            pltpu.VMEM((TOK, 4096), BF16),
            pltpu.VMEM((TOK, 4096), BF16),
            pltpu.VMEM((TOK, 1024), BF16),
            pltpu.VMEM((LP, 1024), F32),
        ],
        scratch_shapes=[
            pltpu.VMEM((TOK, 4096), BF16),
            pltpu.VMEM((TOK, 4096), BF16),
            pltpu.VMEM((TOK, 1024), BF16),
            pltpu.VMEM((TOK, TOK), F32),
            pltpu.VMEM((NP, TOK, HEAD), BF16),
            pltpu.VMEM((NP, LP, TOK), BF16),
            pltpu.VMEM((HEADS, TOK, TOK), F32),
            pltpu.VMEM((HEADS, TOK, TOK), F32),
            pltpu.VMEM((HEADS, 8, TOK), F32),
            pltpu.VMEM((2, KVH, LP, WIDE), BF16),
            pltpu.VMEM((KVH, HEAD, NP * LP + TOK), BF16),
            pltpu.VMEM((KVH, HEAD, NP * LP + TOK), BF16),
            pltpu.VMEM((HEADS, LP, TOK), BF16),
            pltpu.VMEM((HEADS, LP, TOK), BF16),
            pltpu.VMEM((LP, WIDE), F32),
            pltpu.VMEM((LP, WIDE), F32),
            pltpu.VMEM((KVH, TOK, HEAD), F32),
            pltpu.VMEM((KVH, TOK, HEAD), F32),
            pltpu.VMEM((N_RESP, CH, HALF), BF16),
            pltpu.VMEM((N_DP - 1, NP, CH, HALF), BF16),
            pltpu.VMEM((N_DP, NP, CH, HALF), BF16),
            pltpu.VMEM((KVH, CH, WIDE), BF16),
            pltpu.VMEM((KVH, 2, LP, WIDE), BF16),
            pltpu.VMEM((N_RESP - 1, KVH, CH, WIDE), BF16),
            pltpu.VMEM((NP, KVH, CH, HEAD), BF16),
            pltpu.VMEM((N_DP, NP, KVH, CH, HEAD), BF16),
            pltpu.VMEM((N_RESP - 1, KVH, CH, HEAD), BF16),
            pltpu.VMEM((N_RESP, KVH, CH, HEAD), BF16),
            pltpu.SMEM((N_RESP,), jnp.int32),
            dma((3,)),
            dma(peers), dma(peers),
            dma(row_peers), dma(row_peers),
            dma((KVH,) + peers), dma((KVH,) + peers),
            dma((KVH,) + peers), dma((KVH,) + peers),
            dma(row_peers), dma(row_peers),
            dma(peers), dma(peers),
        ],
        compiler_params=pltpu.CompilerParams(
            collective_id=0, has_side_effects=True, vmem_limit_bytes=50 * 2 ** 20
        ),
        name="grouped_attention",
    )(
        queries[0], cotangent[0], response_kv[0], prompt_kv[0, 0],
        resp_lengths[0], resp_prompt[0], owners.T,
    )
    attn_out, grad_queries, grad_response, grad_prompt = outs
    return attn_out[None], grad_queries[None], grad_response[None], grad_prompt[None, None]


def solution(mesh):
    placed = (
        P("dp", "resp", None),
        P("dp", "resp", None),
        P("dp", "resp", None),
        P("dp", "resp", None, None),
        P("dp", "resp", None),
        P("dp", "resp", None),
        P(),
    )
    return jax.shard_map(
        local,
        mesh=mesh,
        in_specs=placed,
        out_specs=(
            P("dp", "resp", None),
            P("dp", "resp", None),
            P("dp", "resp", None),
            P("dp", "resp", None, None),
        ),
        check_vma=False,
    )
```

```python
import jax
import jax.numpy as jnp
from jax import lax
from jax.experimental import pallas as pl
from jax.experimental.pallas import tpu as pltpu
from jax.sharding import PartitionSpec as P

F32 = jnp.float32
BF16 = jnp.bfloat16
HEAD = 128
QPK = 8
KVH = 4
TOK = 256
LP = 128
NP = 4
HALF = KVH * HEAD
NEG = -1e30
SCALE = HEAD ** -0.5
EXP2_SCALE = SCALE * 1.4426950408889634

NN = (((1,), (0,)), ((), ()))


def dot(a, b, dims):
    return lax.dot_general(a, b, dims, preferred_element_type=F32)


def cols(index, width=HEAD):
    return pl.ds(pl.multiple_of(index * width, width), width)


def build_masks(len_ref, prm_ref, bias, qmask, lmask):
    def slot_ids(place):
        resp = jnp.full(place.shape, -1, jnp.int32)
        prompt = jnp.full(place.shape, -1, jnp.int32)
        start = jnp.int32(0)
        for i in range(4):
            end = start + len_ref[0, i]
            inside = (place >= start) & (place < end)
            resp = jnp.where(inside, i, resp)
            prompt = jnp.where(inside, prm_ref[0, i], prompt)
            start = end
        return resp, prompt

    keys = lax.broadcasted_iota(jnp.int32, (TOK, TOK), 0)
    slots = lax.broadcasted_iota(jnp.int32, (TOK, TOK), 1)
    key_resp, _ = slot_ids(keys)
    slot_resp, _ = slot_ids(slots)
    allowed = (key_resp == slot_resp) & (keys <= slots) & (slot_resp >= 0)
    bias[...] = jnp.where(allowed, 0.0, NEG)
    _, by_row = slot_ids(lax.broadcasted_iota(jnp.int32, (TOK, HEAD), 0))
    _, by_lane = slot_ids(lax.broadcasted_iota(jnp.int32, (LP, TOK), 1))
    for j in range(NP):
        qmask[j] = jnp.where(by_row == j, 1.0, 0.0).astype(BF16)
        lmask[j] = jnp.where(by_lane == j, 1.0, 0.0).astype(BF16)


def self_scores(n, q_ref, do_ref, kv_ref, bias, qt, dt, e_self, dp_self, stat):
    h = n // QPK
    keys = kv_ref[:, cols(h)]
    values = kv_ref[:, cols(h + KVH)]
    q = q_ref[:, cols(n)].T
    do = do_ref[:, cols(n)].T
    qt[n] = q
    dt[n] = do
    raw = dot(keys, q, NN) + bias[...]
    top = jnp.max(raw, axis=0, keepdims=True)
    e = jnp.exp2((raw - top) * EXP2_SCALE)
    dp = dot(values, do, NN)
    e_self[n] = e
    dp_self[n] = dp
    stat[n, 0:1, :] = top
    stat[n, 1:2, :] = jnp.sum(e, axis=0, keepdims=True)
    stat[n, 2:3, :] = jnp.sum(e * dp, axis=0, keepdims=True)


def prompt_scores(n, q_ref, do_ref, qt, dt, qmask, lmask, kvcat, w_pr, ds_pr, stat):
    h = n // QPK
    q = q_ref[:, cols(n)]
    do = do_ref[:, cols(n)]
    qe = jnp.concatenate([q * qmask[j] for j in range(NP)], axis=1)
    de = jnp.concatenate([do * qmask[j] for j in range(NP)], axis=1)
    raw = dot(kvcat[0, h], jnp.concatenate([qt[n] * lmask[j] for j in range(NP)], axis=0), NN)
    dp = dot(kvcat[1, h], jnp.concatenate([dt[n] * lmask[j] for j in range(NP)], axis=0), NN)
    top_self = stat[n, 0:1, :]
    top = jnp.maximum(jnp.max(raw, axis=0, keepdims=True), top_self)
    e = jnp.exp2((raw - top) * EXP2_SCALE)
    shrink = jnp.exp2((top_self - top) * EXP2_SCALE)
    total = jnp.sum(e, axis=0, keepdims=True) + shrink * stat[n, 1:2, :]
    inverse = 1.0 / total
    delta = (jnp.sum(e * dp, axis=0, keepdims=True) + shrink * stat[n, 2:3, :]) * inverse
    w = e * inverse
    ds = (w * (dp - delta)).astype(BF16)
    w = w.astype(BF16)
    stat[n, 3:4, :] = shrink * inverse
    stat[n, 4:5, :] = delta
    w_pr[n] = w
    ds_pr[n] = ds
    return dot(ds, qe, NN), dot(w, de, NN)


def finish(n, q_ref, do_ref, lmask, kt, vt, e_self, dp_self, w_pr, ds_pr, stat, out_ref, dq_ref):
    h = n // QPK
    w = e_self[n] * stat[n, 3:4, :]
    ds = (w * (dp_self[n] - stat[n, 4:5, :])).astype(BF16)
    w = w.astype(BF16)
    w_all = jnp.concatenate([w_pr[n] * lmask[j] for j in range(NP)] + [w], axis=0)
    ds_all = jnp.concatenate([ds_pr[n] * lmask[j] for j in range(NP)] + [ds], axis=0)
    out = dot(vt[h], w_all, NN).astype(BF16)
    dq = (dot(kt[h], ds_all, NN) * SCALE).astype(BF16)
    out_ref[:, cols(n)] = out.T
    dq_ref[:, cols(n)] = dq.T
    return dot(ds, q_ref[:, cols(n)], NN), dot(w, do_ref[:, cols(n)], NN)


def transposed_tables(kvcat, kv_ref, kt, vt):
    for h in range(KVH):
        for half, table in ((0, kt), (1, vt)):
            for j in range(NP):
                table[h, :, j * LP:(j + 1) * LP] = kvcat[half, h, :, j * HEAD:(j + 1) * HEAD].T
            at = half * HALF + h * HEAD
            table[h, :, NP * LP:] = kv_ref[:, at:at + HEAD].T


N_DP = 8
N_RESP = 16
CH = 16
WIDE = NP * HEAD
HEADS = KVH * QPK
SELF_STEP = 4
PROMPT_STEP = 2
FINISH_STEP = 4
SELF_CUTS = (0, 8, 16, 20, 24, 28, 32)
FINISH_CUTS = (0, 8, 12, 16, 20, 24, 32)
PAIRS = 2
MESH = pl.DeviceIdType.MESH
SPOTS = sorted(range(1, N_RESP), key=lambda s: -(min(s // 4, 4 - s // 4) + min(s % 4, 4 - s % 4)))
LANES = sorted(range(1, N_DP), key=lambda s: -min(s // 2, 4 - s // 2))


def kernel(
    q_hbm, do_hbm, kv_hbm, slot_ref, len_ref, prm_ref, own_ref,
    out_ref, dq_ref, gr_ref, gp_out,
    q_ref, do_ref, kv_ref,
    bias, qmask, lmask, qt, dt, e_self, dp_self, stat, kvcat, kt, vt, w_pr, ds_pr, dk_acc, dv_acc, dks, dvs,
    buf1, send2, got_a, got_b, got_c, got_d, mine, gp, gland, gmine, back_a, back_b, back_c, back_d, send3, fin, inv,
    in_sem, s1, r1, s2, r2, s3, r3, s4, r4, s5, r5, s6, r6,
):
    recv2 = (got_a, got_b, got_c, got_d)
    gland2 = (back_a, back_b, back_c, back_d)
    a = lax.axis_index("dp")
    c = lax.axis_index("resp")
    x, core = a // 2, lax.rem(a, 2)
    z, y = c // 4, lax.rem(c, 4)

    loads = [
        pltpu.make_async_copy(src, dst, in_sem.at[i])
        for i, (src, dst) in enumerate(((kv_hbm, kv_ref), (q_hbm, q_ref), (do_hbm, do_ref)))
    ]
    for load in loads:
        load.start()

    def col_to(s):
        return lax.rem(z + s // 4, 4) * 4 + lax.rem(y + s % 4, 4)

    def col_from(s):
        return lax.rem(z + 4 - s // 4, 4) * 4 + lax.rem(y + 4 - s % 4, 4)

    def row_to(s):
        return lax.rem(x + s // 2, 4) * 2 + lax.rem(core + s % 2, 2)

    def spot_of(column):
        return lax.rem(z + 4 - jnp.right_shift(column, 2), 4) * 4 + lax.rem(y + 4 - jnp.bitwise_and(column, 3), 4)

    def lane_of(row):
        return lax.rem(x + 4 - jnp.right_shift(row, 1), 4) * 2 + lax.rem(core + 2 - jnp.bitwise_and(row, 1), 2)

    def chunk(index):
        half = index // 8
        block = lax.rem(index, 8)
        return half, pl.ds(pl.multiple_of(block * CH, CH), CH)

    def send(src, dst, ssem, rsem, device):
        return pltpu.make_async_remote_copy(
            src_ref=src, dst_ref=dst, send_sem=ssem, recv_sem=rsem, device_id=device, device_id_type=MESH
        )

    barrier = pltpu.get_barrier_semaphore()
    for s in SPOTS:
        pl.semaphore_signal(barrier, inc=1, device_id=(a, col_to(s)), device_id_type=MESH)
    for s in LANES:
        pl.semaphore_signal(barrier, inc=1, device_id=(row_to(s), c), device_id_type=MESH)
    build_masks(len_ref, prm_ref, bias, qmask, lmask)
    pl.semaphore_wait(barrier, len(SPOTS) + len(LANES))

    my_half, my_rows = chunk(c)

    first = []
    for s in SPOTS:
        to = col_to(s)
        half, rows = chunk(to)
        lanes = pl.ds(pl.multiple_of(half * HALF, HALF), HALF)
        copy = send(slot_ref.at[rows, lanes], buf1.at[s], s1.at[s - 1], r1.at[s - 1], (a, to))
        copy.start()
        first.append(copy)
    buf1[0] = slot_ref[my_rows, pl.ds(pl.multiple_of(my_half * HALF, HALF), HALF)]

    @pl.loop(0, N_RESP)
    def _(s):
        device = a * N_RESP + lax.rem(z + s // 4, 4) * 4 + lax.rem(y + lax.rem(s, 4), 4)
        found = [jnp.where(own_ref[k % NP, k // NP] == device, k + 1, 0) for k in range(N_DP * NP)]
        while len(found) > 1:
            found = [jnp.maximum(found[k], found[k + 1]) for k in range(0, len(found), 2)]
        inv[s] = found[0]

    for load in loads:
        load.wait()

    def self_part(lo, hi):
        @pl.loop(lo // SELF_STEP, hi // SELF_STEP)
        def _(i):
            for u in range(SELF_STEP):
                self_scores(i * SELF_STEP + u, q_ref, do_ref, kv_ref, bias, qt, dt, e_self, dp_self, stat)

    self_part(SELF_CUTS[0], SELF_CUTS[1])

    for copy in first:
        copy.wait_recv()
    second = []
    spots = {
        (s, j): spot_of(jnp.bitwise_and(own_ref[j, row_to(s)], N_RESP - 1)) for s in range(N_DP) for j in range(NP)
    }
    for h in range(KVH):
        for s in LANES + [0]:
            for j in range(NP):
                piece = buf1[spots[s, j], :, h * HEAD:(h + 1) * HEAD]
                if s == 0:
                    recv2[h][0, :, j * HEAD:(j + 1) * HEAD] = piece
                else:
                    send2[h, s - 1, :, j * HEAD:(j + 1) * HEAD] = piece
            if s:
                copy = send(
                    send2.at[h, s - 1], recv2[h].at[s], s2.at[h, s - 1], r2.at[h, s - 1], (row_to(s), c)
                )
                copy.start()
                second.append(copy)

    self_part(SELF_CUTS[1], SELF_CUTS[2])

    from_lane = [lane_of(jnp.right_shift(own_ref[j, a], 4)) for j in range(NP)]
    third = []
    for h in range(KVH):
        for copy in second[h * len(LANES):(h + 1) * len(LANES)]:
            copy.wait_recv()
        for j in range(NP):
            at = slice(j * HEAD, (j + 1) * HEAD)
            mine[h, :, at] = recv2[h][from_lane[j], :, at]
        for s in SPOTS:
            copy = send(
                mine.at[h], kvcat.at[my_half, h, my_rows, :], s3.at[h, s - 1], r3.at[h, s - 1], (a, col_to(s))
            )
            copy.start()
            third.append(copy)
        kvcat[my_half, h, my_rows, :] = mine[h]
        self_part(SELF_CUTS[2 + h], SELF_CUTS[3 + h])

    fourth = []
    for h in range(KVH):
        for s in SPOTS:
            half, rows = chunk(col_from(s))
            send(mine.at[h], kvcat.at[half, h, rows, :], s3.at[h, s - 1], r3.at[h, s - 1], (a, col_to(s))).wait_recv()
        dk_acc[...] = jnp.zeros_like(dk_acc)
        dv_acc[...] = jnp.zeros_like(dv_acc)

        @pl.loop(0, QPK // PROMPT_STEP)
        def _(i):
            parts = [
                prompt_scores(
                    h * QPK + i * PROMPT_STEP + u, q_ref, do_ref, qt, dt, qmask, lmask, kvcat, w_pr, ds_pr, stat
                )
                for u in range(PROMPT_STEP)
            ]
            dk_acc[...] += sum(p[0] for p in parts)
            dv_acc[...] += sum(p[1] for p in parts)

        gp[h, 0] = (dk_acc[...] * SCALE).astype(BF16)
        gp[h, 1] = dv_acc[...].astype(BF16)
        for s in SPOTS:
            to = col_to(s)
            half, rows = chunk(to)
            copy = send(gp.at[h, half, rows, :], gland.at[s - 1, h], s4.at[h, s - 1], r4.at[h, s - 1], (a, to))
            copy.start()
            fourth.append(copy)

    transposed_tables(kvcat, kv_ref, kt, vt)
    dks[...] = jnp.zeros_like(dks)
    dvs[...] = jnp.zeros_like(dvs)

    def finish_part(lo, hi):
        @pl.loop(lo // FINISH_STEP, hi // FINISH_STEP)
        def _(i):
            parts = [
                finish(i * FINISH_STEP + u, q_ref, do_ref, lmask, kt, vt, e_self, dp_self, w_pr, ds_pr, stat, out_ref, dq_ref)
                for u in range(FINISH_STEP)
            ]
            h = i * FINISH_STEP // QPK
            dks[h] += sum(p[0] for p in parts)
            dvs[h] += sum(p[1] for p in parts)

    fifth = []
    sixth = []

    def to_owners(p):
        for copy in fifth[p * PAIRS * len(LANES):(p + 1) * PAIRS * len(LANES)]:
            copy.wait_recv()
        for s in SPOTS + [0]:
            number = inv[s]
            at = jnp.maximum(number - 1, 0)
            lane = lane_of(jnp.right_shift(at, 2))
            j = jnp.bitwise_and(at, 3)
            for u in range(PAIRS):
                piece = gland2[p * PAIRS + u][lane, j].astype(F32)
                piece = jnp.where(number > 0, piece, 0.0).astype(BF16)
                if s == 0:
                    fin[p, 0, u] = piece
                else:
                    send3[p, s - 1, u] = piece
            if s:
                copy = send(send3.at[p, s - 1], fin.at[p, s], s6.at[p, s - 1], r6.at[p, s - 1], (a, col_to(s)))
                copy.start()
                sixth.append(copy)

    for h in range(KVH):
        finish_part(FINISH_CUTS[h], FINISH_CUTS[h + 1])
        for copy in fourth[h * len(SPOTS):(h + 1) * len(SPOTS)]:
            copy.wait_recv()
        total = gp[h, my_half, my_rows, :].astype(F32)
        for s in SPOTS:
            total += gland[s - 1, h].astype(F32)
        total = total.astype(BF16)
        for j in range(NP):
            gmine[h, j] = total[:, j * HEAD:(j + 1) * HEAD]
        for s in LANES:
            copy = send(gmine.at[h], gland2[h].at[s], s5.at[h, s - 1], r5.at[h, s - 1], (row_to(s), c))
            copy.start()
            fifth.append(copy)
        gland2[h][0] = gmine[h]
        if h == KVH - 1:
            to_owners(0)
    finish_part(FINISH_CUTS[4], FINISH_CUTS[5])
    to_owners(1)
    finish_part(FINISH_CUTS[5], FINISH_CUTS[6])

    for h in range(KVH):
        gr_ref[:, h * HEAD:(h + 1) * HEAD] = (dks[h] * SCALE).astype(BF16)
        gr_ref[:, HALF + h * HEAD:HALF + (h + 1) * HEAD] = dvs[h].astype(BF16)

    for copy in sixth:
        copy.wait_recv()
    for s in range(N_RESP):
        half, rows = chunk(col_from(s))
        for h in range(KVH):
            lanes = pl.ds(pl.multiple_of(half * HALF + h * HEAD, HEAD), HEAD)
            gp_out[rows, lanes] = fin[h // PAIRS, s, h % PAIRS].astype(F32)

    for copy in first + second + third + fourth + fifth + sixth:
        copy.wait_send()


def local(queries, response_kv, cotangent, prompt_kv, resp_lengths, resp_prompt, owners):
    vm = pl.BlockSpec(memory_space=pltpu.VMEM)
    sm = pl.BlockSpec(memory_space=pltpu.SMEM)
    hbm = pl.BlockSpec(memory_space=pl.ANY)
    peers = (N_RESP - 1,)
    row_peers = (N_DP - 1,)
    dma = pltpu.SemaphoreType.DMA
    outs = pl.pallas_call(
        kernel,
        in_specs=[hbm, hbm, hbm, vm, sm, sm, sm],
        out_specs=[vm] * 4,
        out_shape=[
            pltpu.VMEM((TOK, 4096), BF16),
            pltpu.VMEM((TOK, 4096), BF16),
            pltpu.VMEM((TOK, 1024), BF16),
            pltpu.VMEM((LP, 1024), F32),
        ],
        scratch_shapes=[
            pltpu.VMEM((TOK, 4096), BF16),
            pltpu.VMEM((TOK, 4096), BF16),
            pltpu.VMEM((TOK, 1024), BF16),
            pltpu.VMEM((TOK, TOK), F32),
            pltpu.VMEM((NP, TOK, HEAD), BF16),
            pltpu.VMEM((NP, LP, TOK), BF16),
            pltpu.VMEM((HEADS, HEAD, TOK), BF16),
            pltpu.VMEM((HEADS, HEAD, TOK), BF16),
            pltpu.VMEM((HEADS, TOK, TOK), F32),
            pltpu.VMEM((HEADS, TOK, TOK), F32),
            pltpu.VMEM((HEADS, 8, TOK), F32),
            pltpu.VMEM((2, KVH, LP, WIDE), BF16),
            pltpu.VMEM((KVH, HEAD, NP * LP + TOK), BF16),
            pltpu.VMEM((KVH, HEAD, NP * LP + TOK), BF16),
            pltpu.VMEM((HEADS, LP, TOK), BF16),
            pltpu.VMEM((HEADS, LP, TOK), BF16),
            pltpu.VMEM((LP, WIDE), F32),
            pltpu.VMEM((LP, WIDE), F32),
            pltpu.VMEM((KVH, TOK, HEAD), F32),
            pltpu.VMEM((KVH, TOK, HEAD), F32),
            pltpu.VMEM((N_RESP, CH, HALF), BF16),
            pltpu.VMEM((KVH, N_DP - 1, CH, WIDE), BF16),
            *[pltpu.VMEM((N_DP, CH, WIDE), BF16)] * KVH,
            pltpu.VMEM((KVH, CH, WIDE), BF16),
            pltpu.VMEM((KVH, 2, LP, WIDE), BF16),
            pltpu.VMEM((N_RESP - 1, KVH, CH, WIDE), BF16),
            pltpu.VMEM((KVH, NP, CH, HEAD), BF16),
            *[pltpu.VMEM((N_DP, NP, CH, HEAD), BF16)] * KVH,
            pltpu.VMEM((KVH // PAIRS, N_RESP - 1, PAIRS, CH, HEAD), BF16),
            pltpu.VMEM((KVH // PAIRS, N_RESP, PAIRS, CH, HEAD), BF16),
            pltpu.SMEM((N_RESP,), jnp.int32),
            dma((3,)),
            dma(peers), dma(peers),
            dma((KVH,) + row_peers), dma((KVH,) + row_peers),
            dma((KVH,) + peers), dma((KVH,) + peers),
            dma((KVH,) + peers), dma((KVH,) + peers),
            dma((KVH,) + row_peers), dma((KVH,) + row_peers),
            dma((KVH // PAIRS,) + peers), dma((KVH // PAIRS,) + peers),
        ],
        compiler_params=pltpu.CompilerParams(
            collective_id=0, has_side_effects=True, vmem_limit_bytes=50 * 2 ** 20
        ),
        name="grouped_attention",
    )(
        queries[0], cotangent[0], response_kv[0], prompt_kv[0, 0],
        resp_lengths[0], resp_prompt[0], owners.T,
    )
    attn_out, grad_queries, grad_response, grad_prompt = outs
    return attn_out[None], grad_queries[None], grad_response[None], grad_prompt[None, None]


def solution(mesh):
    placed = (
        P("dp", "resp", None),
        P("dp", "resp", None),
        P("dp", "resp", None),
        P("dp", "resp", None, None),
        P("dp", "resp", None),
        P("dp", "resp", None),
        P(),
    )
    return jax.shard_map(
        local,
        mesh=mesh,
        in_specs=placed,
        out_specs=(
            P("dp", "resp", None),
            P("dp", "resp", None),
            P("dp", "resp", None),
            P("dp", "resp", None, None),
        ),
        check_vma=False,
    )
```

```python
import jax
import jax.numpy as jnp
from jax import lax
from jax.experimental import pallas as pl
from jax.experimental.pallas import tpu as pltpu
from jax.sharding import PartitionSpec as P

F32 = jnp.float32
BF16 = jnp.bfloat16
HEAD = 128
QPK = 8
KVH = 4
TOK = 256
LP = 128
NP = 4
HALF = KVH * HEAD
NEG = -1e30
SCALE = HEAD ** -0.5
EXP2_SCALE = SCALE * 1.4426950408889634

NN = (((1,), (0,)), ((), ()))


def dot(a, b, dims):
    return lax.dot_general(a, b, dims, preferred_element_type=F32)


def cols(index, width=HEAD):
    return pl.ds(pl.multiple_of(index * width, width), width)


def build_masks(len_ref, prm_ref, bias, qmask, lmask):
    def slot_ids(place):
        resp = jnp.full(place.shape, -1, jnp.int32)
        prompt = jnp.full(place.shape, -1, jnp.int32)
        start = jnp.int32(0)
        for i in range(4):
            end = start + len_ref[0, i]
            inside = (place >= start) & (place < end)
            resp = jnp.where(inside, i, resp)
            prompt = jnp.where(inside, prm_ref[0, i], prompt)
            start = end
        return resp, prompt

    keys = lax.broadcasted_iota(jnp.int32, (TOK, TOK), 0)
    slots = lax.broadcasted_iota(jnp.int32, (TOK, TOK), 1)
    key_resp, _ = slot_ids(keys)
    slot_resp, _ = slot_ids(slots)
    allowed = (key_resp == slot_resp) & (keys <= slots) & (slot_resp >= 0)
    bias[...] = jnp.where(allowed, 0.0, NEG)
    _, by_row = slot_ids(lax.broadcasted_iota(jnp.int32, (TOK, HEAD), 0))
    _, by_lane = slot_ids(lax.broadcasted_iota(jnp.int32, (LP, TOK), 1))
    for j in range(NP):
        qmask[j] = jnp.where(by_row == j, 1.0, 0.0).astype(BF16)
        lmask[j] = jnp.where(by_lane == j, 1.0, 0.0).astype(BF16)


def self_scores(n, q_ref, do_ref, kv_ref, bias, qt, dt, e_self, dp_self, stat):
    h = n // QPK
    keys = kv_ref[:, cols(h)]
    values = kv_ref[:, cols(h + KVH)]
    q = q_ref[:, cols(n)].T
    do = do_ref[:, cols(n)].T
    qt[n] = q
    dt[n] = do
    raw = dot(keys, q, NN) + bias[...]
    top = jnp.max(raw, axis=0, keepdims=True)
    e = jnp.exp2((raw - top) * EXP2_SCALE)
    dp = dot(values, do, NN)
    e_self[n] = e
    dp_self[n] = dp
    stat[n, 0:1, :] = top
    stat[n, 1:2, :] = jnp.sum(e, axis=0, keepdims=True)
    stat[n, 2:3, :] = jnp.sum(e * dp, axis=0, keepdims=True)


def prompt_scores(n, q_ref, do_ref, qt, dt, qmask, lmask, kvcat, w_pr, ds_pr, stat):
    h = n // QPK
    q = q_ref[:, cols(n)]
    do = do_ref[:, cols(n)]
    qe = jnp.concatenate([q * qmask[j] for j in range(NP)], axis=1)
    de = jnp.concatenate([do * qmask[j] for j in range(NP)], axis=1)
    raw = dot(kvcat[0, h], jnp.concatenate([qt[n] * lmask[j] for j in range(NP)], axis=0), NN)
    dp = dot(kvcat[1, h], jnp.concatenate([dt[n] * lmask[j] for j in range(NP)], axis=0), NN)
    top_self = stat[n, 0:1, :]
    top = jnp.maximum(jnp.max(raw, axis=0, keepdims=True), top_self)
    e = jnp.exp2((raw - top) * EXP2_SCALE)
    shrink = jnp.exp2((top_self - top) * EXP2_SCALE)
    total = jnp.sum(e, axis=0, keepdims=True) + shrink * stat[n, 1:2, :]
    inverse = 1.0 / total
    delta = (jnp.sum(e * dp, axis=0, keepdims=True) + shrink * stat[n, 2:3, :]) * inverse
    w = e * inverse
    ds = (w * (dp - delta)).astype(BF16)
    w = w.astype(BF16)
    stat[n, 3:4, :] = shrink * inverse
    stat[n, 4:5, :] = delta
    w_pr[n] = w
    ds_pr[n] = ds
    return dot(ds, qe, NN), dot(w, de, NN)


def finish(n, q_ref, do_ref, lmask, kt, vt, e_self, dp_self, w_pr, ds_pr, stat, out_ref, dq_ref):
    h = n // QPK
    w = e_self[n] * stat[n, 3:4, :]
    ds = (w * (dp_self[n] - stat[n, 4:5, :])).astype(BF16)
    w = w.astype(BF16)
    w_all = jnp.concatenate([w_pr[n] * lmask[j] for j in range(NP)] + [w], axis=0)
    ds_all = jnp.concatenate([ds_pr[n] * lmask[j] for j in range(NP)] + [ds], axis=0)
    out = dot(vt[h], w_all, NN).astype(BF16)
    dq = (dot(kt[h], ds_all, NN) * SCALE).astype(BF16)
    out_ref[:, cols(n)] = out.T
    dq_ref[:, cols(n)] = dq.T
    return dot(ds, q_ref[:, cols(n)], NN), dot(w, do_ref[:, cols(n)], NN)


def transposed_tables(kvcat, kv_ref, kt, vt):
    for h in range(KVH):
        for half, table in ((0, kt), (1, vt)):
            for j in range(NP):
                table[h, :, j * LP:(j + 1) * LP] = kvcat[half, h, :, j * HEAD:(j + 1) * HEAD].T
            at = half * HALF + h * HEAD
            table[h, :, NP * LP:] = kv_ref[:, at:at + HEAD].T


N_DP = 8
N_RESP = 16
CH = 16
WIDE = NP * HEAD
HEADS = KVH * QPK
SELF_STEP = 4
PROMPT_STEP = 2
FINISH_STEP = 4
SELF_CUTS = (0, 8, 16, 20, 24, 28, 32)
FINISH_CUTS = (0, 8, 12, 16, 20, 24, 32)
PAIRS = 2
MESH = pl.DeviceIdType.MESH
SPOTS = sorted(range(1, N_RESP), key=lambda s: -(min(s // 4, 4 - s // 4) + min(s % 4, 4 - s % 4)))
LANES = sorted(range(1, N_DP), key=lambda s: -min(s // 2, 4 - s // 2))


def kernel(
    q_hbm, do_hbm, kv_hbm, slot_ref, len_ref, prm_ref, own_ref,
    out_ref, dq_ref, gr_ref, gp_out,
    q_ref, do_ref, kv_ref,
    bias, qmask, lmask, qt, dt, e_self, dp_self, stat, kvcat, kt, vt, w_pr, ds_pr, dk_acc, dv_acc, dks, dvs,
    buf1, send2, got_a, got_b, got_c, got_d, mine, gp, gland, gmine, back_a, back_b, back_c, back_d, send3, fin, inv,
    in_sem, s1, r1, s2, r2, s3, r3, s4, r4, s5, r5, s6, r6,
):
    recv2 = (got_a, got_b, got_c, got_d)
    gland2 = (back_a, back_b, back_c, back_d)
    a = lax.axis_index("dp")
    c = lax.axis_index("resp")
    x, core = a // 2, lax.rem(a, 2)
    z, y = c // 4, lax.rem(c, 4)

    loads = [
        pltpu.make_async_copy(src, dst, in_sem.at[i])
        for i, (src, dst) in enumerate(((kv_hbm, kv_ref), (q_hbm, q_ref), (do_hbm, do_ref)))
    ]
    for load in loads:
        load.start()

    def col_to(s):
        return lax.rem(z + s // 4, 4) * 4 + lax.rem(y + s % 4, 4)

    def col_from(s):
        return lax.rem(z + 4 - s // 4, 4) * 4 + lax.rem(y + 4 - s % 4, 4)

    def row_to(s):
        return lax.rem(x + s // 2, 4) * 2 + lax.rem(core + s % 2, 2)

    def spot_of(column):
        return lax.rem(z + 4 - jnp.right_shift(column, 2), 4) * 4 + lax.rem(y + 4 - jnp.bitwise_and(column, 3), 4)

    def lane_of(row):
        return lax.rem(x + 4 - jnp.right_shift(row, 1), 4) * 2 + lax.rem(core + 2 - jnp.bitwise_and(row, 1), 2)

    def chunk(index):
        half = index // 8
        block = lax.rem(index, 8)
        return half, pl.ds(pl.multiple_of(block * CH, CH), CH)

    def send(src, dst, ssem, rsem, device):
        return pltpu.make_async_remote_copy(
            src_ref=src, dst_ref=dst, send_sem=ssem, recv_sem=rsem, device_id=device, device_id_type=MESH
        )

    def arrived(ref, rsem):
        send(ref, ref, s1, rsem, (a, col_to(1))).wait_recv()

    def gone(ref, ssem):
        send(ref, ref, ssem, r1, (a, col_to(1))).wait_send()

    barrier = pltpu.get_barrier_semaphore()
    for s in SPOTS:
        pl.semaphore_signal(barrier, inc=1, device_id=(a, col_to(s)), device_id_type=MESH)
    for s in LANES:
        pl.semaphore_signal(barrier, inc=1, device_id=(row_to(s), c), device_id_type=MESH)
    build_masks(len_ref, prm_ref, bias, qmask, lmask)
    pl.semaphore_wait(barrier, len(SPOTS) + len(LANES))

    my_half, my_rows = chunk(c)

    for s in SPOTS:
        to = col_to(s)
        half, rows = chunk(to)
        lanes = pl.ds(pl.multiple_of(half * HALF, HALF), HALF)
        copy = send(slot_ref.at[rows, lanes], buf1.at[s], s1, r1, (a, to))
        copy.start()
    buf1[0] = slot_ref[my_rows, pl.ds(pl.multiple_of(my_half * HALF, HALF), HALF)]

    @pl.loop(0, N_RESP)
    def _(s):
        device = a * N_RESP + lax.rem(z + s // 4, 4) * 4 + lax.rem(y + lax.rem(s, 4), 4)
        found = [jnp.where(own_ref[k % NP, k // NP] == device, k + 1, 0) for k in range(N_DP * NP)]
        while len(found) > 1:
            found = [jnp.maximum(found[k], found[k + 1]) for k in range(0, len(found), 2)]
        inv[s] = found[0]

    for load in loads:
        load.wait()

    def self_part(lo, hi):
        @pl.loop(lo // SELF_STEP, hi // SELF_STEP)
        def _(i):
            for u in range(SELF_STEP):
                self_scores(i * SELF_STEP + u, q_ref, do_ref, kv_ref, bias, qt, dt, e_self, dp_self, stat)

    self_part(SELF_CUTS[0], SELF_CUTS[1])

    arrived(buf1.at[pl.ds(1, N_RESP - 1)], r1)
    spots = {
        (s, j): spot_of(jnp.bitwise_and(own_ref[j, row_to(s)], N_RESP - 1)) for s in range(N_DP) for j in range(NP)
    }
    for h in range(KVH):
        for s in LANES + [0]:
            for j in range(NP):
                piece = buf1[spots[s, j], :, h * HEAD:(h + 1) * HEAD]
                if s == 0:
                    recv2[h][0, :, j * HEAD:(j + 1) * HEAD] = piece
                else:
                    send2[h, s - 1, :, j * HEAD:(j + 1) * HEAD] = piece
            if s:
                copy = send(send2.at[h, s - 1], recv2[h].at[s], s2, r2.at[h], (row_to(s), c))
                copy.start()

    self_part(SELF_CUTS[1], SELF_CUTS[2])

    from_lane = [lane_of(jnp.right_shift(own_ref[j, a], 4)) for j in range(NP)]
    for h in range(KVH):
        arrived(recv2[h].at[pl.ds(1, N_DP - 1)], r2.at[h])
        for j in range(NP):
            at = slice(j * HEAD, (j + 1) * HEAD)
            mine[h, :, at] = recv2[h][from_lane[j], :, at]
        for s in SPOTS:
            copy = send(mine.at[h], kvcat.at[my_half, h, my_rows, :], s3, r3.at[h], (a, col_to(s)))
            copy.start()
        kvcat[my_half, h, my_rows, :] = mine[h]
        self_part(SELF_CUTS[2 + h], SELF_CUTS[3 + h])

    for h in range(KVH):
        arrived(gland.at[h], r3.at[h])
        dk_acc[...] = jnp.zeros_like(dk_acc)
        dv_acc[...] = jnp.zeros_like(dv_acc)

        @pl.loop(0, QPK // PROMPT_STEP)
        def _(i):
            parts = [
                prompt_scores(
                    h * QPK + i * PROMPT_STEP + u, q_ref, do_ref, qt, dt, qmask, lmask, kvcat, w_pr, ds_pr, stat
                )
                for u in range(PROMPT_STEP)
            ]
            dk_acc[...] += sum(p[0] for p in parts)
            dv_acc[...] += sum(p[1] for p in parts)

        gp[h, 0] = (dk_acc[...] * SCALE).astype(BF16)
        gp[h, 1] = dv_acc[...].astype(BF16)
        for s in SPOTS:
            to = col_to(s)
            half, rows = chunk(to)
            copy = send(gp.at[h, half, rows, :], gland.at[h, s - 1], s4, r4.at[h], (a, to))
            copy.start()

    transposed_tables(kvcat, kv_ref, kt, vt)
    dks[...] = jnp.zeros_like(dks)
    dvs[...] = jnp.zeros_like(dvs)

    def finish_part(lo, hi):
        @pl.loop(lo // FINISH_STEP, hi // FINISH_STEP)
        def _(i):
            parts = [
                finish(i * FINISH_STEP + u, q_ref, do_ref, lmask, kt, vt, e_self, dp_self, w_pr, ds_pr, stat, out_ref, dq_ref)
                for u in range(FINISH_STEP)
            ]
            h = i * FINISH_STEP // QPK
            dks[h] += sum(p[0] for p in parts)
            dvs[h] += sum(p[1] for p in parts)

    def to_owners(p):
        for u in range(PAIRS):
            arrived(gland2[p * PAIRS + u].at[pl.ds(1, N_DP - 1)], r5.at[p * PAIRS + u])
        for s in SPOTS + [0]:
            number = inv[s]
            at = jnp.maximum(number - 1, 0)
            lane = lane_of(jnp.right_shift(at, 2))
            j = jnp.bitwise_and(at, 3)
            for u in range(PAIRS):
                piece = gland2[p * PAIRS + u][lane, j].astype(F32)
                piece = jnp.where(number > 0, piece, 0.0).astype(BF16)
                if s == 0:
                    fin[p, 0, u] = piece
                else:
                    send3[p, s - 1, u] = piece
            if s:
                copy = send(send3.at[p, s - 1], fin.at[p, s], s6, r6.at[p], (a, col_to(s)))
                copy.start()

    for h in range(KVH):
        finish_part(FINISH_CUTS[h], FINISH_CUTS[h + 1])
        arrived(gland.at[h], r4.at[h])
        total = gp[h, my_half, my_rows, :].astype(F32)
        for s in SPOTS:
            total += gland[h, s - 1].astype(F32)
        total = total.astype(BF16)
        for j in range(NP):
            gmine[h, j] = total[:, j * HEAD:(j + 1) * HEAD]
        for s in LANES:
            copy = send(gmine.at[h], gland2[h].at[s], s5, r5.at[h], (row_to(s), c))
            copy.start()
        gland2[h][0] = gmine[h]
        if h == KVH - 1:
            to_owners(0)
    finish_part(FINISH_CUTS[4], FINISH_CUTS[5])
    to_owners(1)
    finish_part(FINISH_CUTS[5], FINISH_CUTS[6])

    for h in range(KVH):
        gr_ref[:, h * HEAD:(h + 1) * HEAD] = (dks[h] * SCALE).astype(BF16)
        gr_ref[:, HALF + h * HEAD:HALF + (h + 1) * HEAD] = dvs[h].astype(BF16)

    for p in range(KVH // PAIRS):
        arrived(fin.at[p, pl.ds(1, N_RESP - 1)], r6.at[p])
    for s in range(N_RESP):
        half, rows = chunk(col_from(s))
        for h in range(KVH):
            lanes = pl.ds(pl.multiple_of(half * HALF + h * HEAD, HEAD), HEAD)
            gp_out[rows, lanes] = fin[h // PAIRS, s, h % PAIRS].astype(F32)

    gone(buf1.at[pl.ds(1, N_RESP - 1)], s1)
    gone(send2, s2)
    gone(gland, s3)
    gone(gland, s4)
    gone(send2, s5)
    gone(send3, s6)


def local(queries, response_kv, cotangent, prompt_kv, resp_lengths, resp_prompt, owners):
    vm = pl.BlockSpec(memory_space=pltpu.VMEM)
    sm = pl.BlockSpec(memory_space=pltpu.SMEM)
    hbm = pl.BlockSpec(memory_space=pl.ANY)
    dma = pltpu.SemaphoreType.DMA
    outs = pl.pallas_call(
        kernel,
        in_specs=[hbm, hbm, hbm, vm, sm, sm, sm],
        out_specs=[vm] * 4,
        out_shape=[
            pltpu.VMEM((TOK, 4096), BF16),
            pltpu.VMEM((TOK, 4096), BF16),
            pltpu.VMEM((TOK, 1024), BF16),
            pltpu.VMEM((LP, 1024), F32),
        ],
        scratch_shapes=[
            pltpu.VMEM((TOK, 4096), BF16),
            pltpu.VMEM((TOK, 4096), BF16),
            pltpu.VMEM((TOK, 1024), BF16),
            pltpu.VMEM((TOK, TOK), F32),
            pltpu.VMEM((NP, TOK, HEAD), BF16),
            pltpu.VMEM((NP, LP, TOK), BF16),
            pltpu.VMEM((HEADS, HEAD, TOK), BF16),
            pltpu.VMEM((HEADS, HEAD, TOK), BF16),
            pltpu.VMEM((HEADS, TOK, TOK), F32),
            pltpu.VMEM((HEADS, TOK, TOK), F32),
            pltpu.VMEM((HEADS, 8, TOK), F32),
            pltpu.VMEM((2, KVH, LP, WIDE), BF16),
            pltpu.VMEM((KVH, HEAD, NP * LP + TOK), BF16),
            pltpu.VMEM((KVH, HEAD, NP * LP + TOK), BF16),
            pltpu.VMEM((HEADS, LP, TOK), BF16),
            pltpu.VMEM((HEADS, LP, TOK), BF16),
            pltpu.VMEM((LP, WIDE), F32),
            pltpu.VMEM((LP, WIDE), F32),
            pltpu.VMEM((KVH, TOK, HEAD), F32),
            pltpu.VMEM((KVH, TOK, HEAD), F32),
            pltpu.VMEM((N_RESP, CH, HALF), BF16),
            pltpu.VMEM((KVH, N_DP - 1, CH, WIDE), BF16),
            *[pltpu.VMEM((N_DP, CH, WIDE), BF16)] * KVH,
            pltpu.VMEM((KVH, CH, WIDE), BF16),
            pltpu.VMEM((KVH, 2, LP, WIDE), BF16),
            pltpu.VMEM((KVH, N_RESP - 1, CH, WIDE), BF16),
            pltpu.VMEM((KVH, NP, CH, HEAD), BF16),
            *[pltpu.VMEM((N_DP, NP, CH, HEAD), BF16)] * KVH,
            pltpu.VMEM((KVH // PAIRS, N_RESP - 1, PAIRS, CH, HEAD), BF16),
            pltpu.VMEM((KVH // PAIRS, N_RESP, PAIRS, CH, HEAD), BF16),
            pltpu.SMEM((N_RESP,), jnp.int32),
            dma((3,)),
            dma, dma,
            dma, dma((KVH,)),
            dma, dma((KVH,)),
            dma, dma((KVH,)),
            dma, dma((KVH,)),
            dma, dma((KVH // PAIRS,)),
        ],
        compiler_params=pltpu.CompilerParams(
            collective_id=0, has_side_effects=True, vmem_limit_bytes=50 * 2 ** 20
        ),
        name="grouped_attention",
    )(
        queries[0], cotangent[0], response_kv[0], prompt_kv[0, 0],
        resp_lengths[0], resp_prompt[0], owners.T,
    )
    attn_out, grad_queries, grad_response, grad_prompt = outs
    return attn_out[None], grad_queries[None], grad_response[None], grad_prompt[None, None]


def solution(mesh):
    placed = (
        P("dp", "resp", None),
        P("dp", "resp", None),
        P("dp", "resp", None),
        P("dp", "resp", None, None),
        P("dp", "resp", None),
        P("dp", "resp", None),
        P(),
    )
    return jax.shard_map(
        local,
        mesh=mesh,
        in_specs=placed,
        out_specs=(
            P("dp", "resp", None),
            P("dp", "resp", None),
            P("dp", "resp", None),
            P("dp", "resp", None, None),
        ),
        check_vma=False,
    )
```

```python
import jax
import jax.numpy as jnp
from jax import lax
from jax.experimental import pallas as pl
from jax.experimental.pallas import tpu as pltpu
from jax.sharding import PartitionSpec as P

F32 = jnp.float32
BF16 = jnp.bfloat16
HEAD = 128
QPK = 8
KVH = 4
TOK = 256
LP = 128
NP = 4
HALF = KVH * HEAD
NEG = -1e30
SCALE = HEAD ** -0.5
EXP2_SCALE = SCALE * 1.4426950408889634

NN = (((1,), (0,)), ((), ()))


def dot(a, b, dims):
    return lax.dot_general(a, b, dims, preferred_element_type=F32)


def cols(index, width=HEAD):
    return pl.ds(pl.multiple_of(index * width, width), width)


def build_masks(len_ref, prm_ref, bias, qmask, lmask):
    def slot_ids(place):
        resp = jnp.full(place.shape, -1, jnp.int32)
        prompt = jnp.full(place.shape, -1, jnp.int32)
        start = jnp.int32(0)
        for i in range(4):
            end = start + len_ref[0, i]
            inside = (place >= start) & (place < end)
            resp = jnp.where(inside, i, resp)
            prompt = jnp.where(inside, prm_ref[0, i], prompt)
            start = end
        return resp, prompt

    keys = lax.broadcasted_iota(jnp.int32, (TOK, TOK), 0)
    slots = lax.broadcasted_iota(jnp.int32, (TOK, TOK), 1)
    key_resp, _ = slot_ids(keys)
    slot_resp, _ = slot_ids(slots)
    allowed = (key_resp == slot_resp) & (keys <= slots) & (slot_resp >= 0)
    bias[...] = jnp.where(allowed, 0.0, NEG)
    _, by_row = slot_ids(lax.broadcasted_iota(jnp.int32, (TOK, HEAD), 0))
    _, by_lane = slot_ids(lax.broadcasted_iota(jnp.int32, (LP, TOK), 1))
    for j in range(NP):
        qmask[j] = jnp.where(by_row == j, 1.0, 0.0).astype(BF16)
        lmask[j] = jnp.where(by_lane == j, 1.0, 0.0).astype(BF16)


def self_scores(n, q_ref, do_ref, kv_ref, bias, qt, dt, e_self, dp_self, stat):
    h = n // QPK
    keys = kv_ref[:, cols(h)]
    values = kv_ref[:, cols(h + KVH)]
    q = q_ref[:, cols(n)].T
    do = do_ref[:, cols(n)].T
    qt[n] = q
    dt[n] = do
    raw = dot(keys, q, NN) + bias[...]
    top = jnp.max(raw, axis=0, keepdims=True)
    e = jnp.exp2((raw - top) * EXP2_SCALE)
    dp = dot(values, do, NN)
    e_self[n] = e
    dp_self[n] = dp
    stat[n, 0:1, :] = top
    stat[n, 1:2, :] = jnp.sum(e, axis=0, keepdims=True)
    stat[n, 2:3, :] = jnp.sum(e * dp, axis=0, keepdims=True)


def prompt_scores(n, q_ref, do_ref, qt, dt, qmask, lmask, kvcat, w_pr, ds_pr, stat):
    h = n // QPK
    q = q_ref[:, cols(n)]
    do = do_ref[:, cols(n)]
    qe = jnp.concatenate([q * qmask[j] for j in range(NP)], axis=1)
    de = jnp.concatenate([do * qmask[j] for j in range(NP)], axis=1)
    raw = dot(kvcat[0, h], jnp.concatenate([qt[n] * lmask[j] for j in range(NP)], axis=0), NN)
    dp = dot(kvcat[1, h], jnp.concatenate([dt[n] * lmask[j] for j in range(NP)], axis=0), NN)
    top_self = stat[n, 0:1, :]
    top = jnp.maximum(jnp.max(raw, axis=0, keepdims=True), top_self)
    e = jnp.exp2((raw - top) * EXP2_SCALE)
    shrink = jnp.exp2((top_self - top) * EXP2_SCALE)
    total = jnp.sum(e, axis=0, keepdims=True) + shrink * stat[n, 1:2, :]
    inverse = 1.0 / total
    delta = (jnp.sum(e * dp, axis=0, keepdims=True) + shrink * stat[n, 2:3, :]) * inverse
    w = e * inverse
    ds = (w * (dp - delta)).astype(BF16)
    w = w.astype(BF16)
    stat[n, 3:4, :] = shrink * inverse
    stat[n, 4:5, :] = delta
    w_pr[n] = w
    ds_pr[n] = ds
    return dot(ds, qe, NN), dot(w, de, NN)


def finish(n, q_ref, do_ref, lmask, kt, vt, e_self, dp_self, w_pr, ds_pr, stat, out_ref, dq_ref):
    h = n // QPK
    w = e_self[n] * stat[n, 3:4, :]
    ds = (w * (dp_self[n] - stat[n, 4:5, :])).astype(BF16)
    w = w.astype(BF16)
    w_all = jnp.concatenate([w_pr[n] * lmask[j] for j in range(NP)] + [w], axis=0)
    ds_all = jnp.concatenate([ds_pr[n] * lmask[j] for j in range(NP)] + [ds], axis=0)
    out = dot(vt[h], w_all, NN).astype(BF16)
    dq = (dot(kt[h], ds_all, NN) * SCALE).astype(BF16)
    out_ref[:, cols(n)] = out.T
    dq_ref[:, cols(n)] = dq.T
    return dot(ds, q_ref[:, cols(n)], NN), dot(w, do_ref[:, cols(n)], NN)


def transposed_tables(kvcat, kv_ref, kt, vt):
    for h in range(KVH):
        for half, table in ((0, kt), (1, vt)):
            for j in range(NP):
                table[h, :, j * LP:(j + 1) * LP] = kvcat[half, h, :, j * HEAD:(j + 1) * HEAD].T
            at = half * HALF + h * HEAD
            table[h, :, NP * LP:] = kv_ref[:, at:at + HEAD].T


N_DP = 8
N_RESP = 16
CH = 16
WIDE = NP * HEAD
HEADS = KVH * QPK
SELF_STEP = 4
PROMPT_STEP = 2
FINISH_STEP = 4
SELF_CUTS = (0, 8, 16, 20, 24, 28, 32)
FINISH_CUTS = (0, 8, 12, 16, 20, 24, 32)
PAIRS = 2
MESH = pl.DeviceIdType.MESH
SPOTS = sorted(range(1, N_RESP), key=lambda s: -(min(s // 4, 4 - s // 4) + min(s % 4, 4 - s % 4)))
LANES = sorted(range(1, N_DP), key=lambda s: -min(s // 2, 4 - s // 2))


def kernel(
    q_hbm, do_hbm, kv_hbm, slot_hbm, len_ref, prm_ref, own_ref,
    out_ref, dq_ref, gr_ref, gp_out,
    q_ref, do_ref, kv_ref, slot_ref,
    bias, qmask, lmask, qt, dt, e_self, dp_self, stat, kvcat, kt, vt, w_pr, ds_pr, dk_acc, dv_acc, dks, dvs,
    buf1, send2, pair_a, pair_b, got_a, got_b, mine, gp, gland, gmine, back_a, back_b, back_c, back_d, send3, fin, inv,
    in_sem, s0, r0, s1, r1, s2, r2, s3, r3, s4, r4, s5, r5, s6, r6,
):
    pair = (pair_a, pair_b)
    recv2 = (got_a, got_b)
    gland2 = (back_a, back_b, back_c, back_d)
    a = lax.axis_index("dp")
    c = lax.axis_index("resp")
    x, core = a // 2, lax.rem(a, 2)
    z, y = c // 4, lax.rem(c, 4)

    loads = [
        pltpu.make_async_copy(src, dst, in_sem.at[i])
        for i, (src, dst) in enumerate(((slot_hbm, slot_ref), (kv_hbm, kv_ref), (q_hbm, q_ref), (do_hbm, do_ref)))
    ]
    for load in loads:
        load.start()

    xs = [lax.rem(x + i, 4) for i in range(4)]
    ks = [core, 1 - core]
    zs = [lax.rem(z + i, 4) for i in range(4)]
    ys = [lax.rem(y + i, 4) for i in range(4)]
    halves = [v // 2 for v in zs]
    blocks = [(v - 2 * w) * 4 for v, w in zip(zs, halves)]

    def col_to(s):
        return zs[s // 4] * 4 + ys[s % 4]

    def row_to(s):
        return xs[s // 2] * 2 + ks[s % 2]

    def spot_of(column):
        dz = jnp.bitwise_and(z + 4 - jnp.right_shift(column, 2), 3)
        return dz * 4 + jnp.bitwise_and(y + 4 - jnp.bitwise_and(column, 3), 3)

    def lane_of(px, pk):
        return jnp.bitwise_and(x + 4 - px, 3) * 2 + jnp.bitwise_and(core + 2 - pk, 1)

    def chunk(dz, dy):
        return halves[dz % 4], pl.ds(pl.multiple_of((blocks[dz % 4] + ys[dy % 4]) * CH, CH), CH)

    def chunk_to(s):
        return chunk(s // 4, s % 4)

    def chunk_from(s):
        return chunk(-(s // 4), -(s % 4))

    def send(src, dst, ssem, rsem, device):
        return pltpu.make_async_remote_copy(
            src_ref=src, dst_ref=dst, send_sem=ssem, recv_sem=rsem, device_id=device, device_id_type=MESH
        )

    def arrived(ref, rsem):
        send(ref, ref, s1, rsem, (a, col_to(1))).wait_recv()

    def gone(ref, ssem):
        send(ref, ref, ssem, r1, (a, col_to(1))).wait_send()

    barrier = pltpu.get_barrier_semaphore()
    for s in SPOTS:
        pl.semaphore_signal(barrier, inc=1, device_id=(a, col_to(s)), device_id_type=MESH)
    for s in LANES:
        pl.semaphore_signal(barrier, inc=1, device_id=(row_to(s), c), device_id_type=MESH)
    build_masks(len_ref, prm_ref, bias, qmask, lmask)
    pl.semaphore_wait(barrier, len(SPOTS) + len(LANES))
    loads[0].wait()

    my_half, my_rows = chunk(0, 0)

    for s in SPOTS:
        to = col_to(s)
        half, rows = chunk_to(s)
        lanes = pl.ds(pl.multiple_of(half * HALF, HALF), HALF)
        copy = send(slot_ref.at[rows, lanes], buf1.at[s], s1, r1, (a, to))
        copy.start()
    buf1[0] = slot_ref[my_rows, pl.ds(pl.multiple_of(my_half * HALF, HALF), HALF)]

    @pl.loop(0, N_RESP)
    def _(s):
        device = a * N_RESP + lax.rem(z + s // 4, 4) * 4 + lax.rem(y + lax.rem(s, 4), 4)
        found = [jnp.where(own_ref[k % NP, k // NP] == device, k + 1, 0) for k in range(N_DP * NP)]
        while len(found) > 1:
            found = [jnp.maximum(found[k], found[k + 1]) for k in range(0, len(found), 2)]
        inv[s] = found[0]

    for load in loads[1:]:
        load.wait()

    def self_part(lo, hi):
        @pl.loop(lo // SELF_STEP, hi // SELF_STEP)
        def _(i):
            for u in range(SELF_STEP):
                self_scores(i * SELF_STEP + u, q_ref, do_ref, kv_ref, bias, qt, dt, e_self, dp_self, stat)

    self_part(SELF_CUTS[0], SELF_CUTS[1])

    arrived(buf1.at[pl.ds(1, N_RESP - 1)], r1)
    for u in range(2):
        lanes = pl.ds(pl.multiple_of((ks[1] + 2 * u) * HEAD, HEAD), HEAD)
        send(buf1.at[:, :, lanes], pair[u].at[core], s0, r0.at[u], (row_to(1), c)).start()
    for u in range(2):
        pair[u][core] = buf1[:, :, pl.ds(pl.multiple_of((core + 2 * u) * HEAD, HEAD), HEAD)]
    owned = {}
    for s in range(N_DP):
        for j in range(NP):
            owner = own_ref[j, row_to(s)]
            owned[s, j] = jnp.bitwise_and(jnp.right_shift(owner, 4), 1), spot_of(jnp.bitwise_and(owner, N_RESP - 1))
    for u in range(2):
        arrived(pair[u].at[0], r0.at[u])
        for s in LANES + [0]:
            for j in range(NP):
                piece = pair[u][owned[s, j][0], owned[s, j][1]]
                if s == 0:
                    recv2[u][0, :, j * HEAD:(j + 1) * HEAD] = piece
                else:
                    send2[u, s - 1, :, j * HEAD:(j + 1) * HEAD] = piece
            if s:
                send(send2.at[u, s - 1], recv2[u].at[s], s2, r2.at[u], (row_to(s), c)).start()

    self_part(SELF_CUTS[1], SELF_CUTS[2])

    from_chip = [jnp.right_shift(own_ref[j, a], 5) for j in range(NP)]
    for h in range(KVH):
        u, k = h // 2, h % 2
        if k == 0:
            arrived(recv2[u].at[pl.ds(1, N_DP - 1)], r2.at[u])
        for j in range(NP):
            at = slice(j * HEAD, (j + 1) * HEAD)
            mine[h, :, at] = recv2[u][lane_of(from_chip[j], k), :, at]
        for s in SPOTS:
            send(mine.at[h], kvcat.at[my_half, h, my_rows, :], s3, r3.at[h], (a, col_to(s))).start()
        kvcat[my_half, h, my_rows, :] = mine[h]
        self_part(SELF_CUTS[2 + h], SELF_CUTS[3 + h])

    for h in range(KVH):
        arrived(gland.at[h], r3.at[h])
        dk_acc[...] = jnp.zeros_like(dk_acc)
        dv_acc[...] = jnp.zeros_like(dv_acc)

        @pl.loop(0, QPK // PROMPT_STEP)
        def _(i):
            parts = [
                prompt_scores(
                    h * QPK + i * PROMPT_STEP + u, q_ref, do_ref, qt, dt, qmask, lmask, kvcat, w_pr, ds_pr, stat
                )
                for u in range(PROMPT_STEP)
            ]
            dk_acc[...] += sum(p[0] for p in parts)
            dv_acc[...] += sum(p[1] for p in parts)

        gp[h, 0] = (dk_acc[...] * SCALE).astype(BF16)
        gp[h, 1] = dv_acc[...].astype(BF16)
        for s in SPOTS:
            to = col_to(s)
            half, rows = chunk_to(s)
            copy = send(gp.at[h, half, rows, :], gland.at[h, s - 1], s4, r4.at[h], (a, to))
            copy.start()

    transposed_tables(kvcat, kv_ref, kt, vt)
    dks[...] = jnp.zeros_like(dks)
    dvs[...] = jnp.zeros_like(dvs)

    def finish_part(lo, hi):
        @pl.loop(lo // FINISH_STEP, hi // FINISH_STEP)
        def _(i):
            parts = [
                finish(i * FINISH_STEP + u, q_ref, do_ref, lmask, kt, vt, e_self, dp_self, w_pr, ds_pr, stat, out_ref, dq_ref)
                for u in range(FINISH_STEP)
            ]
            h = i * FINISH_STEP // QPK
            dks[h] += sum(p[0] for p in parts)
            dvs[h] += sum(p[1] for p in parts)

    def to_owners(p):
        for u in range(PAIRS):
            arrived(gland2[p * PAIRS + u].at[pl.ds(1, N_DP - 1)], r5.at[p * PAIRS + u])
        for s in SPOTS + [0]:
            number = inv[s]
            at = jnp.maximum(number - 1, 0)
            lane = lane_of(jnp.right_shift(at, 3), jnp.bitwise_and(jnp.right_shift(at, 2), 1))
            j = jnp.bitwise_and(at, 3)
            for u in range(PAIRS):
                piece = gland2[p * PAIRS + u][lane, j].astype(F32)
                piece = jnp.where(number > 0, piece, 0.0).astype(BF16)
                if s == 0:
                    fin[p, 0, u] = piece
                else:
                    send3[p, s - 1, u] = piece
            if s:
                copy = send(send3.at[p, s - 1], fin.at[p, s], s6, r6.at[p], (a, col_to(s)))
                copy.start()

    for h in range(KVH):
        finish_part(FINISH_CUTS[h], FINISH_CUTS[h + 1])
        arrived(gland.at[h], r4.at[h])
        total = gp[h, my_half, my_rows, :].astype(F32)
        for s in SPOTS:
            total += gland[h, s - 1].astype(F32)
        total = total.astype(BF16)
        for j in range(NP):
            gmine[h, j] = total[:, j * HEAD:(j + 1) * HEAD]
        for s in LANES:
            copy = send(gmine.at[h], gland2[h].at[s], s5, r5.at[h], (row_to(s), c))
            copy.start()
        gland2[h][0] = gmine[h]
        if h == KVH - 1:
            to_owners(0)
    finish_part(FINISH_CUTS[4], FINISH_CUTS[5])
    to_owners(1)
    finish_part(FINISH_CUTS[5], FINISH_CUTS[6])

    for h in range(KVH):
        gr_ref[:, h * HEAD:(h + 1) * HEAD] = (dks[h] * SCALE).astype(BF16)
        gr_ref[:, HALF + h * HEAD:HALF + (h + 1) * HEAD] = dvs[h].astype(BF16)

    for p in range(KVH // PAIRS):
        arrived(fin.at[p, pl.ds(1, N_RESP - 1)], r6.at[p])
    for s in range(N_RESP):
        half, rows = chunk_from(s)
        for h in range(KVH):
            lanes = pl.ds(pl.multiple_of(half * HALF + h * HEAD, HEAD), HEAD)
            gp_out[rows, lanes] = fin[h // PAIRS, s, h % PAIRS].astype(F32)

    gone(pair_a, s0)
    gone(buf1.at[pl.ds(1, N_RESP - 1)], s1)
    gone(send2, s2)
    gone(gland, s3)
    gone(gland, s4)
    gone(gland.at[pl.ds(0, 2), pl.ds(0, 2 * (N_DP - 1))], s5)
    gone(send3, s6)


def store_kernel(*refs):
    sems = refs[8]
    copies = [pltpu.make_async_copy(refs[i], refs[4 + i], sems.at[i]) for i in range(4)]
    for copy in copies:
        copy.start()
    for copy in copies:
        copy.wait()


def local(queries, response_kv, cotangent, prompt_kv, resp_lengths, resp_prompt, owners):
    vm = pl.BlockSpec(memory_space=pltpu.VMEM)
    sm = pl.BlockSpec(memory_space=pltpu.SMEM)
    hbm = pl.BlockSpec(memory_space=pl.ANY)
    dma = pltpu.SemaphoreType.DMA
    outs = pl.pallas_call(
        kernel,
        in_specs=[hbm, hbm, hbm, hbm, sm, sm, sm],
        out_specs=[vm] * 4,
        out_shape=[
            pltpu.VMEM((TOK, 4096), BF16),
            pltpu.VMEM((TOK, 4096), BF16),
            pltpu.VMEM((TOK, 1024), BF16),
            pltpu.VMEM((LP, 1024), F32),
        ],
        scratch_shapes=[
            pltpu.VMEM((TOK, 4096), BF16),
            pltpu.VMEM((TOK, 4096), BF16),
            pltpu.VMEM((TOK, 1024), BF16),
            pltpu.VMEM((LP, 1024), BF16),
            pltpu.VMEM((TOK, TOK), F32),
            pltpu.VMEM((NP, TOK, HEAD), BF16),
            pltpu.VMEM((NP, LP, TOK), BF16),
            pltpu.VMEM((HEADS, HEAD, TOK), BF16),
            pltpu.VMEM((HEADS, HEAD, TOK), BF16),
            pltpu.VMEM((HEADS, TOK, TOK), F32),
            pltpu.VMEM((HEADS, TOK, TOK), F32),
            pltpu.VMEM((HEADS, 8, TOK), F32),
            pltpu.VMEM((2, KVH, LP, WIDE), BF16),
            pltpu.VMEM((KVH, HEAD, NP * LP + TOK), BF16),
            pltpu.VMEM((KVH, HEAD, NP * LP + TOK), BF16),
            pltpu.VMEM((HEADS, LP, TOK), BF16),
            pltpu.VMEM((HEADS, LP, TOK), BF16),
            pltpu.VMEM((LP, WIDE), F32),
            pltpu.VMEM((LP, WIDE), F32),
            pltpu.VMEM((KVH, TOK, HEAD), F32),
            pltpu.VMEM((KVH, TOK, HEAD), F32),
            pltpu.VMEM((N_RESP, CH, HALF), BF16),
            pltpu.VMEM((2, N_DP - 1, CH, WIDE), BF16),
            *[pltpu.VMEM((2, N_RESP, CH, HEAD), BF16)] * 2,
            *[pltpu.VMEM((N_DP, CH, WIDE), BF16)] * 2,
            pltpu.VMEM((KVH, CH, WIDE), BF16),
            pltpu.VMEM((KVH, 2, LP, WIDE), BF16),
            pltpu.VMEM((KVH, N_RESP - 1, CH, WIDE), BF16),
            pltpu.VMEM((KVH, NP, CH, HEAD), BF16),
            *[pltpu.VMEM((N_DP, NP, CH, HEAD), BF16)] * KVH,
            pltpu.VMEM((KVH // PAIRS, N_RESP - 1, PAIRS, CH, HEAD), BF16),
            pltpu.VMEM((KVH // PAIRS, N_RESP, PAIRS, CH, HEAD), BF16),
            pltpu.SMEM((N_RESP,), jnp.int32),
            dma((4,)),
            dma, dma((2,)),
            dma, dma,
            dma, dma((2,)),
            dma, dma((KVH,)),
            dma, dma((KVH,)),
            dma, dma((KVH,)),
            dma, dma((KVH // PAIRS,)),
        ],
        compiler_params=pltpu.CompilerParams(
            collective_id=0, has_side_effects=True, vmem_limit_bytes=58 * 2 ** 20
        ),
        name="grouped_attention",
    )(
        queries[0], cotangent[0], response_kv[0], prompt_kv[0, 0],
        resp_lengths[0], resp_prompt[0], owners.T,
    )
    attn_out, grad_queries, grad_response, grad_prompt = pl.pallas_call(
        store_kernel,
        in_specs=[vm] * 4,
        out_specs=[hbm] * 4,
        out_shape=[
            jax.ShapeDtypeStruct((TOK, 4096), BF16),
            jax.ShapeDtypeStruct((TOK, 4096), BF16),
            jax.ShapeDtypeStruct((TOK, 1024), BF16),
            jax.ShapeDtypeStruct((LP, 1024), F32),
        ],
        scratch_shapes=[dma((4,))],
        compiler_params=pltpu.CompilerParams(vmem_limit_bytes=2 ** 20),
        name="store_outputs",
    )(*[pltpu.with_memory_space_constraint(out, pltpu.VMEM) for out in outs])
    return attn_out[None], grad_queries[None], grad_response[None], grad_prompt[None, None]


def solution(mesh):
    placed = (
        P("dp", "resp", None),
        P("dp", "resp", None),
        P("dp", "resp", None),
        P("dp", "resp", None, None),
        P("dp", "resp", None),
        P("dp", "resp", None),
        P(),
    )
    return jax.shard_map(
        local,
        mesh=mesh,
        in_specs=placed,
        out_specs=(
            P("dp", "resp", None),
            P("dp", "resp", None),
            P("dp", "resp", None),
            P("dp", "resp", None, None),
        ),
        check_vma=False,
    )
```

```python
import jax
import jax.numpy as jnp
from jax import lax
from jax.experimental import pallas as pl
from jax.experimental.pallas import tpu as pltpu
from jax.sharding import PartitionSpec as P

F32 = jnp.float32
BF16 = jnp.bfloat16
HEAD = 128
QPK = 8
KVH = 4
TOK = 256
LP = 128
NP = 4
HALF = KVH * HEAD
NEG = -1e30
SCALE = HEAD ** -0.5
EXP2_SCALE = SCALE * 1.4426950408889634

NN = (((1,), (0,)), ((), ()))


def dot(a, b, dims):
    return lax.dot_general(a, b, dims, preferred_element_type=F32)


def cols(index, width=HEAD):
    return pl.ds(pl.multiple_of(index * width, width), width)


def build_masks(len_ref, prm_ref, bias, qmask, lmask):
    def slot_ids(place):
        resp = jnp.full(place.shape, -1, jnp.int32)
        prompt = jnp.full(place.shape, -1, jnp.int32)
        start = jnp.int32(0)
        for i in range(4):
            end = start + len_ref[0, i]
            inside = (place >= start) & (place < end)
            resp = jnp.where(inside, i, resp)
            prompt = jnp.where(inside, prm_ref[0, i], prompt)
            start = end
        return resp, prompt

    keys = lax.broadcasted_iota(jnp.int32, (TOK, TOK), 0)
    slots = lax.broadcasted_iota(jnp.int32, (TOK, TOK), 1)
    key_resp, _ = slot_ids(keys)
    slot_resp, _ = slot_ids(slots)
    allowed = (key_resp == slot_resp) & (keys <= slots) & (slot_resp >= 0)
    bias[...] = jnp.where(allowed, 0.0, NEG)
    _, by_row = slot_ids(lax.broadcasted_iota(jnp.int32, (TOK, HEAD), 0))
    _, by_lane = slot_ids(lax.broadcasted_iota(jnp.int32, (LP, TOK), 1))
    for j in range(NP):
        qmask[j] = jnp.where(by_row == j, 1.0, 0.0).astype(BF16)
        lmask[j] = jnp.where(by_lane == j, 1.0, 0.0).astype(BF16)


def self_scores(n, q_ref, do_ref, kv_ref, bias, qt, dt, e_self, dp_self, stat):
    h = n // QPK
    keys = kv_ref[:, cols(h)]
    values = kv_ref[:, cols(h + KVH)]
    q = q_ref[:, cols(n)].T
    do = do_ref[:, cols(n)].T
    qt[n] = q
    dt[n] = do
    raw = dot(keys, q, NN) + bias[...]
    top = jnp.max(raw, axis=0, keepdims=True)
    e = jnp.exp2((raw - top) * EXP2_SCALE)
    dp = dot(values, do, NN)
    e_self[n] = e
    dp_self[n] = dp
    stat[n, 0:1, :] = top
    stat[n, 1:2, :] = jnp.sum(e, axis=0, keepdims=True)
    stat[n, 2:3, :] = jnp.sum(e * dp, axis=0, keepdims=True)


def prompt_scores(n, q_ref, do_ref, qt, dt, qmask, lmask, kvcat, w_pr, ds_pr, stat):
    h = n // QPK
    q = q_ref[:, cols(n)]
    do = do_ref[:, cols(n)]
    qe = jnp.concatenate([q * qmask[j] for j in range(NP)], axis=1)
    de = jnp.concatenate([do * qmask[j] for j in range(NP)], axis=1)
    raw = dot(kvcat[0, h], jnp.concatenate([qt[n] * lmask[j] for j in range(NP)], axis=0), NN)
    dp = dot(kvcat[1, h], jnp.concatenate([dt[n] * lmask[j] for j in range(NP)], axis=0), NN)
    top_self = stat[n, 0:1, :]
    top = jnp.maximum(jnp.max(raw, axis=0, keepdims=True), top_self)
    e = jnp.exp2((raw - top) * EXP2_SCALE)
    shrink = jnp.exp2((top_self - top) * EXP2_SCALE)
    total = jnp.sum(e, axis=0, keepdims=True) + shrink * stat[n, 1:2, :]
    inverse = 1.0 / total
    delta = (jnp.sum(e * dp, axis=0, keepdims=True) + shrink * stat[n, 2:3, :]) * inverse
    w = e * inverse
    ds = (w * (dp - delta)).astype(BF16)
    w = w.astype(BF16)
    stat[n, 3:4, :] = shrink * inverse
    stat[n, 4:5, :] = delta
    w_pr[n] = w
    ds_pr[n] = ds
    return dot(ds, qe, NN), dot(w, de, NN)


def finish(n, q_ref, do_ref, lmask, kt, vt, e_self, dp_self, w_pr, ds_pr, stat, out_ref, dq_ref):
    h = n // QPK
    w = e_self[n] * stat[n, 3:4, :]
    ds = (w * (dp_self[n] - stat[n, 4:5, :])).astype(BF16)
    w = w.astype(BF16)
    w_all = jnp.concatenate([w_pr[n] * lmask[j] for j in range(NP)] + [w], axis=0)
    ds_all = jnp.concatenate([ds_pr[n] * lmask[j] for j in range(NP)] + [ds], axis=0)
    out = dot(vt[h], w_all, NN).astype(BF16)
    dq = (dot(kt[h], ds_all, NN) * SCALE).astype(BF16)
    out_ref[:, cols(n)] = out.T
    dq_ref[:, cols(n)] = dq.T
    return dot(ds, q_ref[:, cols(n)], NN), dot(w, do_ref[:, cols(n)], NN)


def transposed_tables(kvcat, kv_ref, kt, vt):
    for h in range(KVH):
        for half, table in ((0, kt), (1, vt)):
            for j in range(NP):
                table[h, :, j * LP:(j + 1) * LP] = kvcat[half, h, :, j * HEAD:(j + 1) * HEAD].T
            at = half * HALF + h * HEAD
            table[h, :, NP * LP:] = kv_ref[:, at:at + HEAD].T


N_DP = 8
N_RESP = 16
CH = 16
WIDE = NP * HEAD
HEADS = KVH * QPK
SELF_STEP = 4
PROMPT_STEP = 2
FINISH_STEP = 4
SELF_CUTS = (0, 8, 16, 20, 24, 28, 32)
FINISH_CUTS = (0, 8, 12, 16, 20, 24, 32)
PAIRS = 2
MESH = pl.DeviceIdType.MESH
SPOTS = sorted(range(1, N_RESP), key=lambda s: -(min(s // 4, 4 - s // 4) + min(s % 4, 4 - s % 4)))
MIXED = (10, 9, 6, 11, 14, 5, 15, 7, 13, 8, 2, 4, 1, 12, 3)
LANES = sorted(range(1, N_DP), key=lambda s: -min(s // 2, 4 - s // 2))


def kernel(
    q_hbm, do_hbm, kv_hbm, slot_hbm, len_ref, prm_ref, own_ref,
    out_ref, dq_ref, gr_ref, gp_out,
    q_ref, do_ref, kv_ref, slot_ref,
    bias, qmask, lmask, qt, dt, e_self, dp_self, stat, kvcat, kt, vt, w_pr, ds_pr, dk_acc, dv_acc, dks, dvs,
    buf1, send2, pair_a, pair_b, got_a, got_b, mine, gp, gland, gmine, back_a, back_b, back_c, back_d, send3, fin, inv,
    in_sem, s0, r0, s1, r1, s2, r2, s3, r3, s4, r4, s5, r5, s6, r6,
):
    pair = (pair_a, pair_b)
    recv2 = (got_a, got_b)
    gland2 = (back_a, back_b, back_c, back_d)
    a = lax.axis_index("dp")
    c = lax.axis_index("resp")
    x, core = a // 2, lax.rem(a, 2)
    z, y = c // 4, lax.rem(c, 4)

    loads = [
        pltpu.make_async_copy(src, dst, in_sem.at[i])
        for i, (src, dst) in enumerate(((slot_hbm, slot_ref), (kv_hbm, kv_ref), (q_hbm, q_ref), (do_hbm, do_ref)))
    ]
    for load in loads:
        load.start()

    xs = [lax.rem(x + i, 4) for i in range(4)]
    ks = [core, 1 - core]
    zs = [lax.rem(z + i, 4) for i in range(4)]
    ys = [lax.rem(y + i, 4) for i in range(4)]
    halves = [v // 2 for v in zs]
    blocks = [(v - 2 * w) * 4 for v, w in zip(zs, halves)]

    def col_to(s):
        return zs[s // 4] * 4 + ys[s % 4]

    def row_to(s):
        return xs[s // 2] * 2 + ks[s % 2]

    def spot_of(column):
        dz = jnp.bitwise_and(z + 4 - jnp.right_shift(column, 2), 3)
        return dz * 4 + jnp.bitwise_and(y + 4 - jnp.bitwise_and(column, 3), 3)

    def lane_of(px, pk):
        return jnp.bitwise_and(x + 4 - px, 3) * 2 + jnp.bitwise_and(core + 2 - pk, 1)

    def chunk(dz, dy):
        return halves[dz % 4], pl.ds(pl.multiple_of((blocks[dz % 4] + ys[dy % 4]) * CH, CH), CH)

    def chunk_to(s):
        return chunk(s // 4, s % 4)

    def chunk_from(s):
        return chunk(-(s // 4), -(s % 4))

    def send(src, dst, ssem, rsem, device):
        return pltpu.make_async_remote_copy(
            src_ref=src, dst_ref=dst, send_sem=ssem, recv_sem=rsem, device_id=device, device_id_type=MESH
        )

    def arrived(ref, rsem):
        send(ref, ref, s1, rsem, (a, col_to(1))).wait_recv()

    def gone(ref, ssem):
        send(ref, ref, ssem, r1, (a, col_to(1))).wait_send()

    barrier = pltpu.get_barrier_semaphore()
    for s in SPOTS:
        pl.semaphore_signal(barrier, inc=1, device_id=(a, col_to(s)), device_id_type=MESH)
    for s in LANES:
        pl.semaphore_signal(barrier, inc=1, device_id=(row_to(s), c), device_id_type=MESH)
    build_masks(len_ref, prm_ref, bias, qmask, lmask)
    pl.semaphore_wait(barrier, len(SPOTS) + len(LANES))
    loads[0].wait()

    my_half, my_rows = chunk(0, 0)

    for s in SPOTS:
        to = col_to(s)
        half, rows = chunk_to(s)
        lanes = pl.ds(pl.multiple_of(half * HALF, HALF), HALF)
        copy = send(slot_ref.at[rows, lanes], buf1.at[s], s1, r1, (a, to))
        copy.start()
    buf1[0] = slot_ref[my_rows, pl.ds(pl.multiple_of(my_half * HALF, HALF), HALF)]

    @pl.loop(0, N_RESP)
    def _(s):
        device = a * N_RESP + lax.rem(z + s // 4, 4) * 4 + lax.rem(y + lax.rem(s, 4), 4)
        found = [jnp.where(own_ref[k % NP, k // NP] == device, k + 1, 0) for k in range(N_DP * NP)]
        while len(found) > 1:
            found = [jnp.maximum(found[k], found[k + 1]) for k in range(0, len(found), 2)]
        inv[s] = found[0]

    for load in loads[1:]:
        load.wait()

    def self_part(lo, hi):
        @pl.loop(lo // SELF_STEP, hi // SELF_STEP)
        def _(i):
            for u in range(SELF_STEP):
                self_scores(i * SELF_STEP + u, q_ref, do_ref, kv_ref, bias, qt, dt, e_self, dp_self, stat)

    self_part(SELF_CUTS[0], SELF_CUTS[1])

    arrived(buf1.at[pl.ds(1, N_RESP - 1)], r1)
    for u in range(2):
        lanes = pl.ds(pl.multiple_of((ks[1] + 2 * u) * HEAD, HEAD), HEAD)
        send(buf1.at[:, :, lanes], pair[u].at[core], s0, r0.at[u], (row_to(1), c)).start()
    for u in range(2):
        pair[u][core] = buf1[:, :, pl.ds(pl.multiple_of((core + 2 * u) * HEAD, HEAD), HEAD)]
    owned = {}
    for s in range(N_DP):
        for j in range(NP):
            owner = own_ref[j, row_to(s)]
            owned[s, j] = jnp.bitwise_and(jnp.right_shift(owner, 4), 1), spot_of(jnp.bitwise_and(owner, N_RESP - 1))
    for u in range(2):
        arrived(pair[u].at[0], r0.at[u])
        for s in LANES + [0]:
            for j in range(NP):
                piece = pair[u][owned[s, j][0], owned[s, j][1]]
                if s == 0:
                    recv2[u][0, :, j * HEAD:(j + 1) * HEAD] = piece
                else:
                    send2[u, s - 1, :, j * HEAD:(j + 1) * HEAD] = piece
            if s:
                send(send2.at[u, s - 1], recv2[u].at[s], s2, r2.at[u], (row_to(s), c)).start()

    self_part(SELF_CUTS[1], SELF_CUTS[2])

    from_chip = [jnp.right_shift(own_ref[j, a], 5) for j in range(NP)]
    for h in range(KVH):
        u, k = h // 2, h % 2
        if k == 0:
            arrived(recv2[u].at[pl.ds(1, N_DP - 1)], r2.at[u])
        for j in range(NP):
            at = slice(j * HEAD, (j + 1) * HEAD)
            mine[h, :, at] = recv2[u][lane_of(from_chip[j], k), :, at]
        for s in MIXED:
            send(mine.at[h], kvcat.at[my_half, h, my_rows, :], s3, r3.at[h], (a, col_to(s))).start()
        kvcat[my_half, h, my_rows, :] = mine[h]
        self_part(SELF_CUTS[2 + h], SELF_CUTS[3 + h])

    for h in range(KVH):
        arrived(gland.at[h], r3.at[h])
        dk_acc[...] = jnp.zeros_like(dk_acc)
        dv_acc[...] = jnp.zeros_like(dv_acc)

        @pl.loop(0, QPK // PROMPT_STEP)
        def _(i):
            parts = [
                prompt_scores(
                    h * QPK + i * PROMPT_STEP + u, q_ref, do_ref, qt, dt, qmask, lmask, kvcat, w_pr, ds_pr, stat
                )
                for u in range(PROMPT_STEP)
            ]
            dk_acc[...] += sum(p[0] for p in parts)
            dv_acc[...] += sum(p[1] for p in parts)

        gp[h, 0] = (dk_acc[...] * SCALE).astype(BF16)
        gp[h, 1] = dv_acc[...].astype(BF16)
        for s in MIXED:
            to = col_to(s)
            half, rows = chunk_to(s)
            copy = send(gp.at[h, half, rows, :], gland.at[h, s - 1], s4, r4.at[h], (a, to))
            copy.start()

    transposed_tables(kvcat, kv_ref, kt, vt)
    dks[...] = jnp.zeros_like(dks)
    dvs[...] = jnp.zeros_like(dvs)

    def finish_part(lo, hi):
        @pl.loop(lo // FINISH_STEP, hi // FINISH_STEP)
        def _(i):
            parts = [
                finish(i * FINISH_STEP + u, q_ref, do_ref, lmask, kt, vt, e_self, dp_self, w_pr, ds_pr, stat, out_ref, dq_ref)
                for u in range(FINISH_STEP)
            ]
            h = i * FINISH_STEP // QPK
            dks[h] += sum(p[0] for p in parts)
            dvs[h] += sum(p[1] for p in parts)

    def to_owners(p):
        for u in range(PAIRS):
            arrived(gland2[p * PAIRS + u].at[pl.ds(1, N_DP - 1)], r5.at[p * PAIRS + u])
        for s in SPOTS + [0]:
            number = inv[s]
            at = jnp.maximum(number - 1, 0)
            lane = lane_of(jnp.right_shift(at, 3), jnp.bitwise_and(jnp.right_shift(at, 2), 1))
            j = jnp.bitwise_and(at, 3)
            for u in range(PAIRS):
                piece = gland2[p * PAIRS + u][lane, j].astype(F32)
                piece = jnp.where(number > 0, piece, 0.0).astype(BF16)
                if s == 0:
                    fin[p, 0, u] = piece
                else:
                    send3[p, s - 1, u] = piece
            if s:
                copy = send(send3.at[p, s - 1], fin.at[p, s], s6, r6.at[p], (a, col_to(s)))
                copy.start()

    for h in range(KVH):
        finish_part(FINISH_CUTS[h], FINISH_CUTS[h + 1])
        if h == KVH - 1:
            to_owners(0)
        arrived(gland.at[h], r4.at[h])
        total = gp[h, my_half, my_rows, :].astype(F32)
        for s in SPOTS:
            total += gland[h, s - 1].astype(F32)
        total = total.astype(BF16)
        for j in range(NP):
            gmine[h, j] = total[:, j * HEAD:(j + 1) * HEAD]
        for s in LANES:
            copy = send(gmine.at[h], gland2[h].at[s], s5, r5.at[h], (row_to(s), c))
            copy.start()
        gland2[h][0] = gmine[h]
    finish_part(FINISH_CUTS[4], FINISH_CUTS[5])
    to_owners(1)
    finish_part(FINISH_CUTS[5], FINISH_CUTS[6])

    for h in range(KVH):
        gr_ref[:, h * HEAD:(h + 1) * HEAD] = (dks[h] * SCALE).astype(BF16)
        gr_ref[:, HALF + h * HEAD:HALF + (h + 1) * HEAD] = dvs[h].astype(BF16)

    for p in range(KVH // PAIRS):
        arrived(fin.at[p, pl.ds(1, N_RESP - 1)], r6.at[p])
    for s in range(N_RESP):
        half, rows = chunk_from(s)
        for h in range(KVH):
            lanes = pl.ds(pl.multiple_of(half * HALF + h * HEAD, HEAD), HEAD)
            gp_out[rows, lanes] = fin[h // PAIRS, s, h % PAIRS].astype(F32)

    gone(pair_a, s0)
    gone(buf1.at[pl.ds(1, N_RESP - 1)], s1)
    gone(send2, s2)
    gone(gland, s3)
    gone(gland, s4)
    gone(gland.at[pl.ds(0, 2), pl.ds(0, 2 * (N_DP - 1))], s5)
    gone(send3, s6)


def store_kernel(*refs):
    sems = refs[8]
    copies = [pltpu.make_async_copy(refs[i], refs[4 + i], sems.at[i]) for i in range(4)]
    for copy in copies:
        copy.start()
    for copy in copies:
        copy.wait()


def local(queries, response_kv, cotangent, prompt_kv, resp_lengths, resp_prompt, owners):
    vm = pl.BlockSpec(memory_space=pltpu.VMEM)
    sm = pl.BlockSpec(memory_space=pltpu.SMEM)
    hbm = pl.BlockSpec(memory_space=pl.ANY)
    dma = pltpu.SemaphoreType.DMA
    outs = pl.pallas_call(
        kernel,
        in_specs=[hbm, hbm, hbm, hbm, sm, sm, sm],
        out_specs=[vm] * 4,
        out_shape=[
            pltpu.VMEM((TOK, 4096), BF16),
            pltpu.VMEM((TOK, 4096), BF16),
            pltpu.VMEM((TOK, 1024), BF16),
            pltpu.VMEM((LP, 1024), F32),
        ],
        scratch_shapes=[
            pltpu.VMEM((TOK, 4096), BF16),
            pltpu.VMEM((TOK, 4096), BF16),
            pltpu.VMEM((TOK, 1024), BF16),
            pltpu.VMEM((LP, 1024), BF16),
            pltpu.VMEM((TOK, TOK), F32),
            pltpu.VMEM((NP, TOK, HEAD), BF16),
            pltpu.VMEM((NP, LP, TOK), BF16),
            pltpu.VMEM((HEADS, HEAD, TOK), BF16),
            pltpu.VMEM((HEADS, HEAD, TOK), BF16),
            pltpu.VMEM((HEADS, TOK, TOK), F32),
            pltpu.VMEM((HEADS, TOK, TOK), F32),
            pltpu.VMEM((HEADS, 8, TOK), F32),
            pltpu.VMEM((2, KVH, LP, WIDE), BF16),
            pltpu.VMEM((KVH, HEAD, NP * LP + TOK), BF16),
            pltpu.VMEM((KVH, HEAD, NP * LP + TOK), BF16),
            pltpu.VMEM((HEADS, LP, TOK), BF16),
            pltpu.VMEM((HEADS, LP, TOK), BF16),
            pltpu.VMEM((LP, WIDE), F32),
            pltpu.VMEM((LP, WIDE), F32),
            pltpu.VMEM((KVH, TOK, HEAD), F32),
            pltpu.VMEM((KVH, TOK, HEAD), F32),
            pltpu.VMEM((N_RESP, CH, HALF), BF16),
            pltpu.VMEM((2, N_DP - 1, CH, WIDE), BF16),
            *[pltpu.VMEM((2, N_RESP, CH, HEAD), BF16)] * 2,
            *[pltpu.VMEM((N_DP, CH, WIDE), BF16)] * 2,
            pltpu.VMEM((KVH, CH, WIDE), BF16),
            pltpu.VMEM((KVH, 2, LP, WIDE), BF16),
            pltpu.VMEM((KVH, N_RESP - 1, CH, WIDE), BF16),
            pltpu.VMEM((KVH, NP, CH, HEAD), BF16),
            *[pltpu.VMEM((N_DP, NP, CH, HEAD), BF16)] * KVH,
            pltpu.VMEM((KVH // PAIRS, N_RESP - 1, PAIRS, CH, HEAD), BF16),
            pltpu.VMEM((KVH // PAIRS, N_RESP, PAIRS, CH, HEAD), BF16),
            pltpu.SMEM((N_RESP,), jnp.int32),
            dma((4,)),
            dma, dma((2,)),
            dma, dma,
            dma, dma((2,)),
            dma, dma((KVH,)),
            dma, dma((KVH,)),
            dma, dma((KVH,)),
            dma, dma((KVH // PAIRS,)),
        ],
        compiler_params=pltpu.CompilerParams(
            collective_id=0, has_side_effects=True, vmem_limit_bytes=58 * 2 ** 20
        ),
        name="grouped_attention",
    )(
        queries[0], cotangent[0], response_kv[0], prompt_kv[0, 0],
        resp_lengths[0], resp_prompt[0], owners.T,
    )
    attn_out, grad_queries, grad_response, grad_prompt = pl.pallas_call(
        store_kernel,
        in_specs=[vm] * 4,
        out_specs=[hbm] * 4,
        out_shape=[
            jax.ShapeDtypeStruct((TOK, 4096), BF16),
            jax.ShapeDtypeStruct((TOK, 4096), BF16),
            jax.ShapeDtypeStruct((TOK, 1024), BF16),
            jax.ShapeDtypeStruct((LP, 1024), F32),
        ],
        scratch_shapes=[dma((4,))],
        compiler_params=pltpu.CompilerParams(vmem_limit_bytes=2 ** 20),
        name="store_outputs",
    )(*[pltpu.with_memory_space_constraint(out, pltpu.VMEM) for out in outs])
    return attn_out[None], grad_queries[None], grad_response[None], grad_prompt[None, None]


def solution(mesh):
    placed = (
        P("dp", "resp", None),
        P("dp", "resp", None),
        P("dp", "resp", None),
        P("dp", "resp", None, None),
        P("dp", "resp", None),
        P("dp", "resp", None),
        P(),
    )
    return jax.shard_map(
        local,
        mesh=mesh,
        in_specs=placed,
        out_specs=(
            P("dp", "resp", None),
            P("dp", "resp", None),
            P("dp", "resp", None),
            P("dp", "resp", None, None),
        ),
        check_vma=False,
    )
```
